512 devices in a mesh: gx: 16 (over y, core), gy: 32 (over z, x).
Axes of the slice: x: 4, y: 8, z: 8, core: 2. Of those that a mesh axis runs over, the one named last changes fastest.
Arguments:
- counts: float32 [4, 256, 512, 512], P(None, 'gx', 'gy'), may hold values from -9000 to 9000, as said below
- spread: float32 [512], replicated, may hold values from 0.5 to 1.5
Outputs:
- scores: float32 [4, 256, 512, 512], P(None, 'gx', 'gy')
The draws below stay inside these ranges and needn't reach their ends.
Inputs may be any that keep to these rules, and one draw needn't show every extreme that they name: Spectra of counts, real-valued; every entry is finite.
All inputs are finite; a program needn't handle non-finite values.
Results may differ from the reference program's by a relative error of at most 0.0003.
Values sent between devices are 32-bit elements; how exact they have to be, the bound alone decides.
A program may use at most 64 MiB of HBM per device.

```python
import math
import jax
import jax.numpy as jnp
from jax import lax

BINS = 512
RADIUS = 2
PLANES = 4
TX = 16
TY = 16
NX = 256
NY = 512


def draw_counts(key, part):
    key = jax.random.fold_in(key, 7)
    key_base = jax.random.fold_in(key, 1)
    key_voxel = jax.random.fold_in(key, 2)
    key_bins = jax.random.fold_in(key, 3)
    key_region = jax.random.fold_in(key, 4)
    base_draw = jax.random.truncated_normal(key_base, -5.0, 5.0, (PLANES, NX, NY, BINS), jnp.float32)
    voxel_scale = jnp.exp(jax.random.uniform(key_voxel, (PLANES, NX, NY, 1), jnp.float32, 0.0, math.log(10.0)))
    bin_scale = jnp.exp(jax.random.uniform(key_bins, (BINS,), jnp.float32, 0.0, math.log(10.0)))
    region = jnp.exp(jax.random.uniform(key_region, (NX // TX, NY // TY, BINS), jnp.float32, 0.0, math.log(10.0)))
    region = jnp.repeat(jnp.repeat(region, TX, axis=0), TY, axis=1)
    slope_x = jnp.sqrt(1.0 + 2.0 * jnp.arange(NX).astype(jnp.float32) / max(NX - 1, 1))[None, :, None, None]
    return base_draw * voxel_scale * bin_scale * region[None] * slope_x


def setup_inputs(seed: int = 0) -> dict:
    seeds = jax.random.split(jax.random.key(seed), 3)
    return {
        "counts": draw_counts(jax.random.fold_in(seeds[2], 71), 0),
        "spread": jnp.clip(jnp.exp(jax.random.uniform(seeds[1], (BINS,), jnp.float32, math.log(0.5), math.log(1.5))), 0.5, 1.5),
    }


def kernel_taps(spread):
    offsets = jnp.arange(-RADIUS, RADIUS + 1).astype(jnp.float32)[:, None]
    profile = jnp.exp(-offsets * offsets / (2.0 * spread[None, :] * spread[None, :]))
    return profile / lax.optimization_barrier(jnp.sum(profile, axis=0, keepdims=True))

def blur_along(padded, taps, along, length):
    result = taps[0] * lax.slice_in_dim(padded, 0, length, axis=along)
    for shift_k in range(1, 2 * RADIUS + 1):
        result = result + taps[shift_k] * lax.slice_in_dim(padded, shift_k, shift_k + length, axis=along)
    return result

def reference(counts, spread):
    taps = kernel_taps(spread)
    padded = jnp.pad(counts, ((0, 0), (RADIUS, RADIUS), (RADIUS, RADIUS), (0, 0)))
    first_pass = blur_along(padded, taps, 1, NX)
    smoothed = blur_along(first_pass, taps, 2, NY)
    rows_all = PLANES * NX * NY
    matrix_y = smoothed.reshape(rows_all, BINS)
    gram = jnp.dot(matrix_y.T.astype(jnp.float32), matrix_y.astype(jnp.float32), precision=lax.Precision.HIGHEST, preferred_element_type=jnp.float32)
    lower = jnp.linalg.cholesky(gram)
    identity = jnp.eye(BINS, dtype=jnp.float32)
    lower_inv = lax.linalg.triangular_solve(lower, identity, left_side=True, lower=True)
    scores = jnp.dot(matrix_y.astype(jnp.float32), lower_inv.T.astype(jnp.float32), precision=lax.Precision.HIGHEST, preferred_element_type=jnp.float32)
    scores = scores * math.sqrt(rows_all)
    return scores.reshape(PLANES, NX, NY, BINS)
```

```python
import math

import jax
import jax.numpy as jnp
from jax import lax
from jax.experimental import pallas as pl
from jax.experimental.pallas import tpu as pltpu
from jax.sharding import PartitionSpec as P

RADIUS = 2
BINS = 512
PLANES = 4
SIDE = 16
CORES = 2
X_CHIPS = 4
Y_CHIPS = 8
Z_CHIPS = 8
F32 = jnp.float32
BF16 = jnp.bfloat16
HIGHEST = lax.Precision.HIGHEST
MESH = pl.DeviceIdType.MESH

BLOCKS = [(i, j) for i in range(4) for j in range(i, 4)]
PACKED = len(BLOCKS) * 128
HALF = PACKED // CORES
QUARTER = HALF // X_CHIPS
EIGHTH = 24
PADDED = EIGHTH * Z_CHIPS
PANEL = 16


def split2(x):
    high = x.astype(BF16)
    return high, (x - high.astype(F32)).astype(BF16)


def split3(x):
    high = x.astype(BF16).astype(F32)
    rest = x - high
    middle = rest.astype(BF16).astype(F32)
    return high, middle, rest - middle


def tap_rows(spread):
    offsets = [float(k) for k in range(-RADIUS, RADIUS + 1)]
    profile = [jnp.exp(-k * k / (2.0 * spread * spread)) for k in offsets]
    total = profile[0]
    for row in profile[1:]:
        total = total + row
    return [row / total for row in profile]


def gram_kernel(
    counts_ref,
    spread_ref,
    gram_ref,
    smooth_ref,
    grid,
    blurred,
    smooth,
    edge_out,
    edge_in,
    corner_out,
    corner_in,
    packed,
    from_core,
    from_x,
    quarter,
    from_z,
    from_y,
    gathered,
    whole,
    load_sems,
    x_send,
    x_recv,
    y_send,
    y_recv,
    c_send,
    c_recv,
    red_send,
    red_recv,
    out_sems,
):
    gx, gy = lax.axis_index("gx"), lax.axis_index("gy")
    nx, ny = CORES * Y_CHIPS, Z_CHIPS * X_CHIPS
    core, y = lax.rem(gx, CORES), gx // CORES
    x, z = lax.rem(gy, X_CHIPS), gy // X_CHIPS

    loads = []
    for p in range(PLANES):
        load = pltpu.make_async_copy(
            counts_ref.at[p],
            grid.at[p, RADIUS : RADIUS + SIDE, 8 : 8 + SIDE, :],
            load_sems.at[p],
        )
        load.start()
        loads.append(load)

    def core_peer():
        return (y * CORES + 1 - core, gy)

    def x_peer(d):
        return (gx, z * X_CHIPS + lax.rem(x + d, X_CHIPS))

    def z_peer(d):
        return (gx, lax.rem(z + d, Z_CHIPS) * X_CHIPS + x)

    def y_peer(d):
        return (lax.rem(y + d, Y_CHIPS) * CORES + core, gy)

    def beside(dx, dy):
        return (lax.rem(gx + dx + nx, nx), lax.rem(gy + dy + ny, ny))

    around = [(dx, dy) for dx in (-1, 0, 1) for dy in (-1, 0, 1) if (dx, dy) != (0, 0)]
    partners = [beside(dx, dy) for dx, dy in around]
    partners += [core_peer()]
    partners += [x_peer(d) for d in range(1, X_CHIPS)]
    partners += [z_peer(d) for d in range(1, Z_CHIPS)]
    partners += [y_peer(d) for d in range(1, Y_CHIPS)]
    barrier = pltpu.get_barrier_semaphore()
    for partner in partners:
        pl.semaphore_signal(barrier, inc=1, device_id=partner, device_id_type=MESH)

    def there(dx, dy):
        inside = None
        for delta, here, size in ((dx, gx, nx), (dy, gy, ny)):
            if delta:
                test = here > 0 if delta < 0 else here < size - 1
                inside = test if inside is None else jnp.logical_and(inside, test)
        return inside

    for p in range(PLANES):
        loads[p].wait()
        for i in range(SIDE):
            row = grid[p, RADIUS + i, 8:16, :]
            edge_out[0, p, 2 * i : 2 * i + 2, :] = row[0:2]
            row2 = grid[p, RADIUS + i, 16:24, :]
            edge_out[1, p, 2 * i : 2 * i + 2, :] = row2[6:8]
        for a, first in ((0, 0), (1, SIDE - 2)):
            for b in (0, 1):
                corner_out[2 * a + b, 4 * p : 4 * p + 4, :] = edge_out[
                    b, p, 2 * first : 2 * first + 4, :
                ]

    pl.semaphore_wait(barrier, len(partners))

    def x_copy(p, side):
        rows = (RADIUS, RADIUS + SIDE - 2)[side]
        lands = (RADIUS + SIDE, 0)[side]
        return pltpu.make_async_remote_copy(
            src_ref=grid.at[p, rows : rows + 2, 8 : 8 + SIDE, :],
            dst_ref=grid.at[p, lands : lands + 2, 8 : 8 + SIDE, :],
            send_sem=x_send.at[p, side],
            recv_sem=x_recv.at[p, side],
            device_id=beside((-1, 1)[side], 0),
            device_id_type=MESH,
        )

    def y_copy(p, side):
        return pltpu.make_async_remote_copy(
            src_ref=edge_out.at[side, p],
            dst_ref=edge_in.at[1 - side, p],
            send_sem=y_send.at[p, side],
            recv_sem=y_recv.at[p, side],
            device_id=beside(0, (-1, 1)[side]),
            device_id_type=MESH,
        )

    def corner_copy(a, b):
        return pltpu.make_async_remote_copy(
            src_ref=corner_out.at[2 * a + b],
            dst_ref=corner_in.at[2 * (1 - a) + 1 - b],
            send_sem=c_send.at[2 * a + b],
            recv_sem=c_recv.at[2 * a + b],
            device_id=beside((-1, 1)[a], (-1, 1)[b]),
            device_id_type=MESH,
        )

    sign = (-1, 1)
    for a in (0, 1):
        for b in (0, 1):

            @pl.when(there(sign[a], sign[b]))
            def _():
                corner_copy(a, b).start()

            @pl.when(jnp.logical_not(there(sign[a], sign[b])))
            def _():
                corner_in[2 * a + b] = jnp.zeros((4 * PLANES, BINS), F32)

    for p in range(PLANES):
        for side in (0, 1):

            @pl.when(there(0, sign[side]))
            def _():
                y_copy(p, side).start()

            @pl.when(there(sign[side], 0))
            def _():
                x_copy(p, side).start()

    for side in (0, 1):

        @pl.when(jnp.logical_not(there(0, sign[side])))
        def _():
            edge_in[side] = jnp.zeros((PLANES, 2 * SIDE, BINS), F32)

        @pl.when(jnp.logical_not(there(sign[side], 0)))
        def _():
            lands = (0, RADIUS + SIDE)[side]
            for p in range(PLANES):
                grid[p, lands : lands + 2, 8 : 8 + SIDE, :] = jnp.zeros((2, SIDE, BINS), F32)

    taps = tap_rows(spread_ref[...])

    for a in (0, 1):
        for b in (0, 1):

            @pl.when(there(sign[1 - a], sign[1 - b]))
            def _():
                corner_copy(a, b).wait_recv()

    keeps = []
    for p in range(PLANES):
        for side in (0, 1):

            @pl.when(there(0, sign[1 - side]))
            def _():
                y_copy(p, side).wait_recv()

            @pl.when(there(sign[1 - side], 0))
            def _():
                x_copy(p, side).wait_recv()

        for b, lands in ((0, 6), (1, 8 + SIDE)):
            for i in range(SIDE):
                grid[p, RADIUS + i, lands : lands + 2, :] = edge_in[b, p, 2 * i : 2 * i + 2, :]
            for a, first in ((0, 0), (1, RADIUS + SIDE)):
                for i in (0, 1):
                    grid[p, first + i, lands : lands + 2, :] = corner_in[
                        2 * a + b, 4 * p + 2 * i : 4 * p + 2 * i + 2, :
                    ]

        def along_x(i, carry, p=p):
            for lo, hi in ((0, 8), (8, 24), (24, 32)):
                total = taps[0] * grid[p, i, lo:hi, :]
                for k in range(1, 2 * RADIUS + 1):
                    total = total + taps[k] * grid[p, i + k, lo:hi, :]
                blurred[i, lo:hi, :] = total
            return carry

        lax.fori_loop(0, SIDE, along_x, 0)

        def along_y(i, carry, p=p):
            total = taps[0] * blurred[i, 6 : 6 + SIDE, :]
            for k in range(1, 2 * RADIUS + 1):
                total = total + taps[k] * blurred[i, 6 + k : 6 + k + SIDE, :]
            at = pl.multiple_of(p * SIDE * SIDE + i * SIDE, SIDE)
            smooth[pl.ds(at, SIDE), :] = total
            return carry

        lax.fori_loop(0, SIDE, along_y, 0)
        rows = slice(p * SIDE * SIDE, (p + 1) * SIDE * SIDE)
        keep = pltpu.make_async_copy(smooth.at[rows], smooth_ref.at[rows], out_sems.at[p])
        keep.start()
        keeps.append(keep)

        high, low = split2(smooth[rows, :])
        left = jnp.concatenate([high, high, low], axis=0)
        right = jnp.concatenate([high, low, high], axis=0)
        at = 0
        for i in range(4):
            part = lax.dot_general(
                left[:, i * 128 : i * 128 + 128],
                right[:, i * 128 :],
                (((0,), (0,)), ((), ())),
                preferred_element_type=F32,
            )
            for j in range(4 - i):
                block = part[:, j * 128 : j * 128 + 128]
                if p == 0:
                    packed[at : at + 128, :] = block
                else:
                    packed[at : at + 128, :] += block
                at += 128

    def send(n, source, target, device):
        copy = pltpu.make_async_remote_copy(
            src_ref=source,
            dst_ref=target,
            send_sem=red_send.at[n],
            recv_sem=red_recv.at[n],
            device_id=device,
            device_id_type=MESH,
        )
        copy.start()
        return copy

    def rows_at(start, size):
        return pl.ds(pl.multiple_of(start, 8), size)

    sent = []
    copy = send(0, packed.at[rows_at((1 - core) * HALF, HALF)], from_core, core_peer())
    sent.append(copy)
    copy.wait_recv()
    mine = core * HALF
    packed[rows_at(mine, HALF), :] += from_core[...]

    copies = [
        send(
            d,
            packed.at[rows_at(mine + lax.rem(x + d, X_CHIPS) * QUARTER, QUARTER)],
            from_x.at[d - 1],
            x_peer(d),
        )
        for d in range(1, X_CHIPS)
    ]
    sent += copies
    quarter[QUARTER:PADDED, :] = jnp.zeros((PADDED - QUARTER, 128), F32)
    for copy in copies:
        copy.wait_recv()
    total = packed[rows_at(mine + x * QUARTER, QUARTER), :]
    for d in range(X_CHIPS - 1):
        total = total + from_x[d]
    quarter[0:QUARTER, :] = total

    copies = [
        send(
            3 + d,
            quarter.at[rows_at(lax.rem(z + d, Z_CHIPS) * EIGHTH, EIGHTH)],
            from_z.at[d - 1],
            z_peer(d),
        )
        for d in range(1, Z_CHIPS)
    ]
    sent += copies
    for copy in copies:
        copy.wait_recv()
    total = quarter[rows_at(z * EIGHTH, EIGHTH), :]
    for d in range(Z_CHIPS - 1):
        total = total + from_z[d]

    from_y[y] = total
    copies = [send(10 + d, from_y.at[y], from_y.at[y], y_peer(d)) for d in range(1, Y_CHIPS)]
    sent += copies
    for copy in copies:
        copy.wait_recv()
    total = from_y[0]
    for d in range(1, Y_CHIPS):
        total = total + from_y[d]

    here = rows_at(z * EIGHTH, EIGHTH)
    gathered[here, :] = total
    copies = [send(17 + d, gathered.at[here], gathered.at[here], z_peer(d)) for d in range(1, Z_CHIPS)]
    sent += copies
    for copy in copies:
        copy.wait_recv()

    here = rows_at(mine + x * QUARTER, QUARTER)
    copies = [
        send(24 + d, gathered.at[0:QUARTER], whole.at[here], x_peer(d)) for d in range(1, X_CHIPS)
    ]
    sent += copies
    whole[here, :] = gathered[0:QUARTER, :]
    for copy in copies:
        copy.wait_recv()

    here = rows_at(mine, HALF)
    copy = send(28, whole.at[here], whole.at[here], core_peer())
    sent.append(copy)
    copy.wait_recv()

    give = pltpu.make_async_copy(whole, gram_ref, out_sems.at[PLANES])
    give.start()
    for copy in sent:
        copy.wait_send()
    for p in range(PLANES):
        for side in (0, 1):

            @pl.when(there(0, sign[side]))
            def _():
                y_copy(p, side).wait_send()

            @pl.when(there(sign[side], 0))
            def _():
                x_copy(p, side).wait_send()

        keeps[p].wait()
    for a in (0, 1):
        for b in (0, 1):

            @pl.when(there(sign[a], sign[b]))
            def _():
                corner_copy(a, b).wait_send()

    give.wait()


def gram_call(counts, spread):
    dma = pltpu.SemaphoreType.DMA
    rows = PLANES * SIDE * SIDE
    return pl.pallas_call(
        gram_kernel,
        out_shape=[
            jax.ShapeDtypeStruct((PACKED, 128), F32),
            jax.ShapeDtypeStruct((rows, BINS), F32),
        ],
        in_specs=[
            pl.BlockSpec(memory_space=pl.ANY),
            pl.BlockSpec(memory_space=pltpu.VMEM),
        ],
        out_specs=[pl.BlockSpec(memory_space=pl.ANY)] * 2,
        scratch_shapes=[
            pltpu.VMEM((PLANES, SIDE + 2 * RADIUS, SIDE + 16, BINS), F32),
            pltpu.VMEM((SIDE, SIDE + 16, BINS), F32),
            pltpu.VMEM((rows, BINS), F32),
            pltpu.VMEM((2, PLANES, 2 * SIDE, BINS), F32),
            pltpu.VMEM((2, PLANES, 2 * SIDE, BINS), F32),
            pltpu.VMEM((4, 4 * PLANES, BINS), F32),
            pltpu.VMEM((4, 4 * PLANES, BINS), F32),
            pltpu.VMEM((PACKED, 128), F32),
            pltpu.VMEM((HALF, 128), F32),
            pltpu.VMEM((X_CHIPS - 1, QUARTER, 128), F32),
            pltpu.VMEM((PADDED, 128), F32),
            pltpu.VMEM((Z_CHIPS - 1, EIGHTH, 128), F32),
            pltpu.VMEM((Y_CHIPS, EIGHTH, 128), F32),
            pltpu.VMEM((PADDED, 128), F32),
            pltpu.VMEM((PACKED, 128), F32),
            dma((PLANES,)),
            dma((PLANES, 2)),
            dma((PLANES, 2)),
            dma((PLANES, 2)),
            dma((PLANES, 2)),
            dma((4,)),
            dma((4,)),
            dma((29,)),
            dma((29,)),
            dma((PLANES + 1,)),
        ],
        compiler_params=pltpu.CompilerParams(
            collective_id=0, has_side_effects=True, vmem_limit_bytes=48 << 20
        ),
    )(counts, spread)


def factor(a_ref, w_ref):
    sublane = lax.broadcasted_iota(jnp.int32, (8, 128), 0)
    lane = lax.broadcasted_iota(jnp.int32, (PANEL, 128), 1)

    def tile(s):
        return slice(s * 128, s * 128 + 128)

    def spread_row(value, i):
        return jnp.broadcast_to(value[i : i + 1, :], (8, 128))

    for t in range(4):
        block = tile(t)

        def panel(n, carry, t=t, block=block):
            here = pl.ds(pl.multiple_of(t * 128 + n * PANEL, PANEL), PANEL)
            tiles = [a_ref[here, tile(s)] for s in range(t, 4)]
            tiles += [w_ref[here, tile(s)] for s in range(t + 1)]
            corner = pltpu.roll(tiles[0], lax.rem(128 - n * PANEL, 128), axis=1)
            column = [
                [
                    jnp.broadcast_to(corner[8 * g : 8 * g + 8, j : j + 1], (8, 128))
                    for g in range(2)
                ]
                for j in range(PANEL)
            ]
            rows = [[value[0:8], value[8:16]] for value in tiles]
            pivots = [jnp.ones((8, 128), F32)] * 2
            for j in range(PANEL):
                h, q = divmod(j, 8)
                pivot = spread_row(column[j][h], q)
                inverse = pl.reciprocal(pivot, approx=False)
                pivots[h] = jnp.where(sublane == q, pivot, pivots[h])
                weight = [None, None]
                for g in range(h, 2):
                    weight[g] = column[j][g] * inverse
                    if g == h:
                        weight[g] = jnp.where(sublane > q, weight[g], 0.0)
                for i in range(j + 1, PANEL):
                    other = spread_row(column[i][h], q)
                    for g in range(h, 2):
                        column[i][g] = column[i][g] - (column[j][g] * other) * inverse
                for value in rows:
                    other = spread_row(value[h], q)
                    for g in range(h, 2):
                        value[g] = value[g] - weight[g] * other
            scale = [lax.rsqrt(value) for value in pivots]
            rows = [
                jnp.concatenate([value[0] * scale[0], value[1] * scale[1]], axis=0)
                for value in rows
            ]
            for m, s in enumerate(range(t, 4)):
                a_ref[here, tile(s)] = rows[m]
            for s in range(t + 1):
                w_ref[here, tile(s)] = rows[4 - t + s]
            high, middle, low = split3(jnp.where(lane >= (n + 1) * PANEL, rows[0], 0.0))
            left = jnp.concatenate([high, high, middle, high, low, middle], axis=0)
            high, middle, low = split3(jnp.concatenate(rows, axis=1))
            right = jnp.concatenate([high, middle, high, low, high, middle], axis=0)
            update = jnp.dot(
                left.T.astype(BF16), right.astype(BF16), preferred_element_type=F32
            )
            for m, s in enumerate(range(t, 4)):
                a_ref[block, tile(s)] -= update[:, tile(m)]
            for s in range(t + 1):
                w_ref[block, tile(s)] -= update[:, tile(4 - t + s)]
            return carry

        lax.fori_loop(0, 128 // PANEL, panel, 0)
        for s in range(t + 1, 4):
            left = a_ref[block, tile(s)].T
            a_ref[tile(s), s * 128 :] -= jnp.dot(
                left, a_ref[block, s * 128 :], precision=HIGHEST, preferred_element_type=F32
            )
            w_ref[tile(s), : (t + 1) * 128] -= jnp.dot(
                left, w_ref[block, : (t + 1) * 128], precision=HIGHEST, preferred_element_type=F32
            )


def whiten_kernel(scale, gram_ref, smooth_ref, scores_ref, a_ref, w_ref, smooth, scores, load_sem, out_sems):
    load = pltpu.make_async_copy(smooth_ref, smooth, load_sem)
    load.start()
    for n, (i, j) in enumerate(BLOCKS):
        a_ref[i * 128 : i * 128 + 128, j * 128 : j * 128 + 128] = gram_ref[n * 128 : n * 128 + 128, :]
    row = lax.broadcasted_iota(jnp.int32, (BINS, BINS), 0)
    column = lax.broadcasted_iota(jnp.int32, (BINS, BINS), 1)
    w_ref[...] = jnp.where(row == column, 1.0, 0.0).astype(F32)
    factor(a_ref, w_ref)
    load.wait()
    weights = w_ref[...] * scale
    high, low = split2(weights)
    top = jnp.concatenate([high[:256, :256], low[:256, :256], high[:256, :256]], axis=1)
    bottom = jnp.concatenate([high[256:], low[256:], high[256:]], axis=1)
    pieces = 4
    size = smooth.shape[0] // pieces
    copies = []
    for n in range(pieces):
        here = slice(n * size, (n + 1) * size)
        high, low = split2(smooth[here, :])
        left = jnp.concatenate([high[:, :256], high[:, :256], low[:, :256]], axis=1)
        scores[here, :256] = lax.dot_general(
            left, top, (((1,), (1,)), ((), ())), preferred_element_type=F32
        )
        left = jnp.concatenate([high, high, low], axis=1)
        scores[here, 256:] = lax.dot_general(
            left, bottom, (((1,), (1,)), ((), ())), preferred_element_type=F32
        )
        copy = pltpu.make_async_copy(scores.at[here], scores_ref.at[here], out_sems.at[n])
        copy.start()
        copies.append(copy)
    for copy in copies:
        copy.wait()


def whiten_call(gram, smooth, scale):
    rows = smooth.shape[0]

    def kernel(*refs):
        whiten_kernel(scale, *refs)

    return pl.pallas_call(
        kernel,
        out_shape=jax.ShapeDtypeStruct((rows, BINS), F32),
        in_specs=[
            pl.BlockSpec(memory_space=pltpu.VMEM),
            pl.BlockSpec(memory_space=pl.ANY),
        ],
        out_specs=pl.BlockSpec(memory_space=pl.ANY),
        scratch_shapes=[
            pltpu.VMEM((BINS, BINS), F32),
            pltpu.VMEM((BINS, BINS), F32),
            pltpu.VMEM((rows, BINS), F32),
            pltpu.VMEM((rows, BINS), F32),
            pltpu.SemaphoreType.DMA,
            pltpu.SemaphoreType.DMA((4,)),
        ],
        compiler_params=pltpu.CompilerParams(vmem_limit_bytes=48 << 20),
    )(gram, smooth)


def local(counts, spread):
    gram, smooth = gram_call(counts, spread.reshape(1, BINS))
    rows_all = smooth.shape[0] * lax.axis_size("gx") * lax.axis_size("gy")
    scores = whiten_call(gram, smooth, math.sqrt(rows_all))
    return scores.reshape(counts.shape)


def solution(mesh):
    in_specs = (P(None, "gx", "gy", None), P())
    out_specs = P(None, "gx", "gy", None)
    return jax.shard_map(local, mesh=mesh, in_specs=in_specs, out_specs=out_specs, check_vma=False)
```

```python
import functools
import math

import jax
import jax.numpy as jnp
from jax import lax
from jax.experimental import pallas as pl
from jax.experimental.pallas import tpu as pltpu
from jax.sharding import PartitionSpec as P

RADIUS = 2
BINS = 512
PLANES = 4
SIDE = 16
CORES = 2
X_CHIPS = 4
Y_CHIPS = 8
Z_CHIPS = 8
F32 = jnp.float32
BF16 = jnp.bfloat16
MESH = pl.DeviceIdType.MESH

BLOCKS = [(i, j) for i in range(4) for j in range(i, 4)]
PACKED = len(BLOCKS) * 128
CHUNKS = [(0, 512), (512, PACKED - 512)]


def shares(rows):
    half = rows // CORES
    quarter = half // X_CHIPS
    eighth = -(-quarter // (8 * Z_CHIPS)) * 8
    return half, quarter, eighth


PANEL = 16
PIECES = 8


def split3(x):
    high = x.astype(BF16)
    rest = x - high.astype(F32)
    middle = rest.astype(BF16)
    return high, middle, (rest - middle.astype(F32)).astype(BF16)


def left_parts(x, axis):
    high, middle, low = split3(x)
    return jnp.concatenate([high, high, middle, high, low, middle], axis=axis)


def right_parts(x, axis):
    high, middle, low = split3(x)
    return jnp.concatenate([high, middle, high, low, high, middle], axis=axis)


def tile(s):
    return slice(s * 128, s * 128 + 128)


def dot(left, right):
    return jnp.dot(left, right, preferred_element_type=F32)


def tap_rows(spread):
    offsets = [float(k) for k in range(-RADIUS, RADIUS + 1)]
    profile = [jnp.exp(-k * k / (2.0 * spread * spread)) for k in offsets]
    total = profile[0]
    for row in profile[1:]:
        total = total + row
    return [row / total for row in profile]


def gram_kernel(
    counts_ref,
    spread_ref,
    gram_ref,
    smooth_ref,
    grid,
    blurred,
    smooth,
    edge_out,
    edge_in,
    corner_out,
    corner_in,
    packed,
    from_core0,
    from_x0,
    quarter0,
    from_z0,
    from_y0,
    gathered0,
    from_core1,
    from_x1,
    quarter1,
    from_z1,
    from_y1,
    gathered1,
    whole,
    taps_in,
    load_sems,
    taps_sem,
    x_send,
    x_recv,
    y_send,
    y_recv,
    c_send,
    c_recv,
    red_send,
    red_recv,
    out_sems,
):
    gx, gy = lax.axis_index("gx"), lax.axis_index("gy")
    nx, ny = CORES * Y_CHIPS, Z_CHIPS * X_CHIPS
    core, y = lax.rem(gx, CORES), gx // CORES
    x, z = lax.rem(gy, X_CHIPS), gy // X_CHIPS

    taps_load = pltpu.make_async_copy(spread_ref, taps_in, taps_sem)
    taps_load.start()
    loads = []
    for p in range(PLANES):
        load = pltpu.make_async_copy(
            counts_ref.at[p],
            grid.at[p, RADIUS : RADIUS + SIDE, 8 : 8 + SIDE, :],
            load_sems.at[p],
        )
        load.start()
        loads.append(load)

    def core_peer():
        return (y * CORES + 1 - core, gy)

    def x_peer(d):
        return (gx, z * X_CHIPS + lax.rem(x + d, X_CHIPS))

    def z_peer(d):
        return (gx, lax.rem(z + d, Z_CHIPS) * X_CHIPS + x)

    def y_peer(d):
        return (lax.rem(y + d, Y_CHIPS) * CORES + core, gy)

    def beside(dx, dy):
        return (lax.rem(gx + dx + nx, nx), lax.rem(gy + dy + ny, ny))

    around = [(dx, dy) for dx in (-1, 0, 1) for dy in (-1, 0, 1) if (dx, dy) != (0, 0)]
    partners = [beside(dx, dy) for dx, dy in around]
    partners += [core_peer()]
    partners += [x_peer(d) for d in range(1, X_CHIPS)]
    partners += [z_peer(d) for d in range(1, Z_CHIPS)]
    partners += [y_peer(d) for d in range(1, Y_CHIPS)]
    barrier = pltpu.get_barrier_semaphore()
    for partner in partners:
        pl.semaphore_signal(barrier, inc=1, device_id=partner, device_id_type=MESH)

    def there(dx, dy):
        inside = None
        for delta, here, size in ((dx, gx, nx), (dy, gy, ny)):
            if delta:
                test = here > 0 if delta < 0 else here < size - 1
                inside = test if inside is None else jnp.logical_and(inside, test)
        return inside

    for p in range(PLANES):
        loads[p].wait()
        for i in range(SIDE):
            row = grid[p, RADIUS + i, 8:16, :]
            edge_out[0, p, 2 * i : 2 * i + 2, :] = row[0:2]
            row2 = grid[p, RADIUS + i, 16:24, :]
            edge_out[1, p, 2 * i : 2 * i + 2, :] = row2[6:8]
        for a, first in ((0, 0), (1, SIDE - 2)):
            for b in (0, 1):
                corner_out[2 * a + b, 4 * p : 4 * p + 4, :] = edge_out[
                    b, p, 2 * first : 2 * first + 4, :
                ]

    pl.semaphore_wait(barrier, len(partners))

    def x_copy(p, side):
        rows = (RADIUS, RADIUS + SIDE - 2)[side]
        lands = (RADIUS + SIDE, 0)[side]
        return pltpu.make_async_remote_copy(
            src_ref=grid.at[p, rows : rows + 2, 8 : 8 + SIDE, :],
            dst_ref=grid.at[p, lands : lands + 2, 8 : 8 + SIDE, :],
            send_sem=x_send.at[p, side],
            recv_sem=x_recv.at[p, side],
            device_id=beside((-1, 1)[side], 0),
            device_id_type=MESH,
        )

    def y_copy(p, side):
        return pltpu.make_async_remote_copy(
            src_ref=edge_out.at[side, p],
            dst_ref=edge_in.at[1 - side, p],
            send_sem=y_send.at[p, side],
            recv_sem=y_recv.at[p, side],
            device_id=beside(0, (-1, 1)[side]),
            device_id_type=MESH,
        )

    def corner_copy(a, b):
        return pltpu.make_async_remote_copy(
            src_ref=corner_out.at[2 * a + b],
            dst_ref=corner_in.at[2 * (1 - a) + 1 - b],
            send_sem=c_send.at[2 * a + b],
            recv_sem=c_recv.at[2 * a + b],
            device_id=beside((-1, 1)[a], (-1, 1)[b]),
            device_id_type=MESH,
        )

    sign = (-1, 1)
    for a in (0, 1):
        for b in (0, 1):

            @pl.when(there(sign[a], sign[b]))
            def _():
                corner_copy(a, b).start()

            @pl.when(jnp.logical_not(there(sign[a], sign[b])))
            def _():
                corner_in[2 * a + b] = jnp.zeros((4 * PLANES, BINS), F32)

    for p in range(PLANES):
        for side in (0, 1):

            @pl.when(there(0, sign[side]))
            def _():
                y_copy(p, side).start()

            @pl.when(there(sign[side], 0))
            def _():
                x_copy(p, side).start()

    for side in (0, 1):

        @pl.when(jnp.logical_not(there(0, sign[side])))
        def _():
            edge_in[side] = jnp.zeros((PLANES, 2 * SIDE, BINS), F32)

        @pl.when(jnp.logical_not(there(sign[side], 0)))
        def _():
            lands = (0, RADIUS + SIDE)[side]
            for p in range(PLANES):
                grid[p, lands : lands + 2, 8 : 8 + SIDE, :] = jnp.zeros((2, SIDE, BINS), F32)

    taps_load.wait()
    taps = tap_rows(taps_in[...])

    for a in (0, 1):
        for b in (0, 1):

            @pl.when(there(sign[1 - a], sign[1 - b]))
            def _():
                corner_copy(a, b).wait_recv()

    def rows_at(start, size):
        return pl.ds(pl.multiple_of(start, 8), size)

    buffers = [
        (from_core0, from_x0, quarter0, from_z0, from_y0, gathered0),
        (from_core1, from_x1, quarter1, from_z1, from_y1, gathered1),
    ]
    sent = []
    gives = []

    def reduction(c):
        first, rows = CHUNKS[c]
        half, fourth, eighth = shares(rows)
        from_core, from_x, quarter, from_z, from_y, gathered = buffers[c]

        def send(n, source, target, device):
            copy = pltpu.make_async_remote_copy(
                src_ref=source,
                dst_ref=target,
                send_sem=red_send.at[c, n],
                recv_sem=red_recv.at[c, n],
                device_id=device,
                device_id_type=MESH,
            )
            copy.start()
            sent.append(copy)
            return copy

        copy = send(
            0, packed.at[rows_at(first + (1 - core) * half, half)], from_core, core_peer()
        )
        if fourth < Z_CHIPS * eighth:
            quarter[fourth:, :] = jnp.zeros((Z_CHIPS * eighth - fourth, 128), F32)
        yield
        copy.wait_recv()
        mine = first + core * half
        packed[rows_at(mine, half), :] += from_core[...]

        copies = [
            send(
                d,
                packed.at[rows_at(mine + lax.rem(x + d, X_CHIPS) * fourth, fourth)],
                from_x.at[d - 1],
                x_peer(d),
            )
            for d in range(1, X_CHIPS)
        ]
        yield
        for copy in copies:
            copy.wait_recv()
        total = packed[rows_at(mine + x * fourth, fourth), :]
        for d in range(X_CHIPS - 1):
            total = total + from_x[d]
        quarter[0:fourth, :] = total

        copies = [
            send(
                3 + d,
                quarter.at[rows_at(lax.rem(z + d, Z_CHIPS) * eighth, eighth)],
                from_z.at[d - 1],
                z_peer(d),
            )
            for d in range(1, Z_CHIPS)
        ]
        yield
        for copy in copies:
            copy.wait_recv()
        total = quarter[rows_at(z * eighth, eighth), :]
        for d in range(Z_CHIPS - 1):
            total = total + from_z[d]

        from_y[y] = total
        copies = [send(10 + d, from_y.at[y], from_y.at[y], y_peer(d)) for d in range(1, Y_CHIPS)]
        yield
        for copy in copies:
            copy.wait_recv()
        total = from_y[0]
        for d in range(1, Y_CHIPS):
            total = total + from_y[d]

        here = rows_at(z * eighth, eighth)
        gathered[here, :] = total
        copies = [
            send(17 + d, gathered.at[here], gathered.at[here], z_peer(d))
            for d in range(1, Z_CHIPS)
        ]
        yield
        for copy in copies:
            copy.wait_recv()
        here = rows_at(mine + x * fourth, fourth)
        copies = [
            send(24 + d, gathered.at[0:fourth], whole.at[here], x_peer(d))
            for d in range(1, X_CHIPS)
        ]
        whole[here, :] = gathered[0:fourth, :]
        yield
        for copy in copies:
            copy.wait_recv()
        here = rows_at(mine, half)
        copy = send(28, whole.at[here], whole.at[here], core_peer())
        yield
        copy.wait_recv()
        give = pltpu.make_async_copy(
            whole.at[first : first + rows], gram_ref.at[first : first + rows], out_sems.at[PLANES + c]
        )
        give.start()
        gives.append(give)

    keeps = []
    for p in range(PLANES):
        for side in (0, 1):

            @pl.when(there(0, sign[1 - side]))
            def _():
                y_copy(p, side).wait_recv()

            @pl.when(there(sign[1 - side], 0))
            def _():
                x_copy(p, side).wait_recv()

        for b, lands in ((0, 6), (1, 8 + SIDE)):
            for i in range(SIDE):
                grid[p, RADIUS + i, lands : lands + 2, :] = edge_in[b, p, 2 * i : 2 * i + 2, :]
            for a, first in ((0, 0), (1, RADIUS + SIDE)):
                for i in (0, 1):
                    grid[p, first + i, lands : lands + 2, :] = corner_in[
                        2 * a + b, 4 * p + 2 * i : 4 * p + 2 * i + 2, :
                    ]

        def along_x(i, carry, p=p):
            for lo, hi in ((0, 8), (8, 24), (24, 32)):
                total = taps[0] * grid[p, i, lo:hi, :]
                for k in range(1, 2 * RADIUS + 1):
                    total = total + taps[k] * grid[p, i + k, lo:hi, :]
                blurred[i, lo:hi, :] = total
            return carry

        lax.fori_loop(0, SIDE, along_x, 0)

        def along_y(i, carry, p=p):
            total = taps[0] * blurred[i, 6 : 6 + SIDE, :]
            for k in range(1, 2 * RADIUS + 1):
                total = total + taps[k] * blurred[i, 6 + k : 6 + k + SIDE, :]
            at = pl.multiple_of(p * SIDE * SIDE + i * SIDE, SIDE)
            smooth[pl.ds(at, SIDE), :] = total
            return carry

        lax.fori_loop(0, SIDE, along_y, 0)
        rows = slice(p * SIDE * SIDE, (p + 1) * SIDE * SIDE)
        keep = pltpu.make_async_copy(smooth.at[rows], smooth_ref.at[rows], out_sems.at[p])
        keep.start()
        keeps.append(keep)

        value = smooth[rows, :]
        left = left_parts(value.T, 1)
        right = right_parts(value, 0)
        at = 0
        for i in range(4):
            part = dot(left[tile(i), :], right[:, i * 128 :])
            for j in range(4 - i):
                block = part[:, tile(j)]
                if p == 0:
                    packed[at : at + 128, :] = block
                else:
                    packed[at : at + 128, :] += block
                at += 128
            if p == PLANES - 1 and i == 0:
                first_chunk = reduction(0)
                next(first_chunk)

    second_chunk = reduction(1)
    next(second_chunk)
    under_way = [first_chunk, second_chunk]
    while under_way:
        under_way = [chunk for chunk in under_way if next(chunk, chunk) is not chunk]
    for copy in sent:
        copy.wait_send()
    for p in range(PLANES):
        for side in (0, 1):

            @pl.when(there(0, sign[side]))
            def _():
                y_copy(p, side).wait_send()

            @pl.when(there(sign[side], 0))
            def _():
                x_copy(p, side).wait_send()

        keeps[p].wait()
    for a in (0, 1):
        for b in (0, 1):

            @pl.when(there(sign[a], sign[b]))
            def _():
                corner_copy(a, b).wait_send()

    for give in gives:
        give.wait()


def gram_call(counts, spread):
    dma = pltpu.SemaphoreType.DMA
    rows = PLANES * SIDE * SIDE
    reduction_buffers = []
    for _, chunk in CHUNKS:
        half, fourth, eighth = shares(chunk)
        for shape in (
            (half,),
            (X_CHIPS - 1, fourth),
            (Z_CHIPS * eighth,),
            (Z_CHIPS - 1, eighth),
            (Y_CHIPS, eighth),
            (Z_CHIPS * eighth,),
        ):
            reduction_buffers.append(pltpu.VMEM((*shape, 128), F32))
    return pl.pallas_call(
        gram_kernel,
        out_shape=[
            jax.ShapeDtypeStruct((PACKED, 128), F32),
            jax.ShapeDtypeStruct((rows, BINS), F32),
        ],
        in_specs=[pl.BlockSpec(memory_space=pl.ANY)] * 2,
        out_specs=[pl.BlockSpec(memory_space=pl.ANY)] * 2,
        scratch_shapes=[
            pltpu.VMEM((PLANES, SIDE + 2 * RADIUS, SIDE + 16, BINS), F32),
            pltpu.VMEM((SIDE, SIDE + 16, BINS), F32),
            pltpu.VMEM((rows, BINS), F32),
            pltpu.VMEM((2, PLANES, 2 * SIDE, BINS), F32),
            pltpu.VMEM((2, PLANES, 2 * SIDE, BINS), F32),
            pltpu.VMEM((4, 4 * PLANES, BINS), F32),
            pltpu.VMEM((4, 4 * PLANES, BINS), F32),
            pltpu.VMEM((PACKED, 128), F32),
            *reduction_buffers,
            pltpu.VMEM((PACKED, 128), F32),
            pltpu.VMEM((1, BINS), F32),
            dma((PLANES,)),
            dma,
            dma((PLANES, 2)),
            dma((PLANES, 2)),
            dma((PLANES, 2)),
            dma((PLANES, 2)),
            dma((4,)),
            dma((4,)),
            dma((2, 29)),
            dma((2, 29)),
            dma((PLANES + 2,)),
        ],
        compiler_params=pltpu.CompilerParams(
            collective_id=0, has_side_effects=True, vmem_limit_bytes=62 << 20
        ),
    )(counts, spread)


def factor_block(t, a_ref, w_ref, parts_ref, work):
    sublane = lax.broadcasted_iota(jnp.int32, (8, 128), 0)
    panels = 128 // PANEL
    width = 4 - t

    def at(s, rows):
        return (a_ref, rows, tile(t + s)) if s < width else (w_ref, rows, slice(0, 128))

    def column_parts(value, first, keep):
        lane = lax.broadcasted_iota(jnp.int32, value.shape, 1)
        column = jnp.take_along_axis(value, first + lane % PANEL, axis=1)
        if keep is not None:
            column = jnp.where(keep, column, 0.0)
        high, middle, low = split3(column)
        high, middle, low = high.astype(F32), middle.astype(F32), low.astype(F32)
        group = lane // PANEL
        value = jnp.where(
            (group == 0) | (group == 1) | (group == 3),
            high,
            jnp.where((group == 2) | (group == 5), middle, jnp.where(group == 4, low, 0.0)),
        )
        return value.astype(BF16)

    def lose(rows, left, right):
        update = dot(left, right)
        for s in range(width + 1):
            ref, at_rows, columns = at(s, rows)
            ref[at_rows, columns] -= update[:, tile(s)]

    for p in range(panels):
        first = t * 128 + p * PANEL
        here = slice(first, first + PANEL)
        rows = []
        for s in range(width + 1):
            ref, at_rows, columns = at(s, here)
            rows.append([ref[first + 8 * g : first + 8 * g + 8, columns] for g in range(2)])
        column = [
            [
                jnp.take_along_axis(
                    rows[0][g], jnp.full((8, 128), p * PANEL + j, jnp.int32), axis=1
                )
                for g in range(2)
            ]
            for j in range(PANEL)
        ]
        factor = [list(value) for value in rows]
        pivots = [jnp.ones((8, 128), F32)] * 2
        inverses = [jnp.ones((8, 128), F32)] * 2
        if 0 < p < panels - 1:
            beyond = slice(first + PANEL, t * 128 + 128)
            left = column_parts(a_ref[beyond, tile(t)], (p - 1) * PANEL, None)
            lose(beyond, left, parts_ref[:, : (width + 1) * 128])
        for j in range(PANEL):
            h, q = divmod(j, 8)
            pivot = jnp.broadcast_to(column[j][h][q : q + 1, :], (8, 128))
            inverse = 1.0 / pivot
            pivots[h] = jnp.where(sublane == q, pivot, pivots[h])
            inverses[h] = jnp.where(sublane == q, inverse, inverses[h])
            weight = [
                (jnp.where(sublane != q, column[j][g], 0.0) if g == h else column[j][g]) * inverse
                for g in range(2)
            ]
            for i in range(j + 1, PANEL):
                other = jnp.broadcast_to(column[i][h][q : q + 1, :], (8, 128))
                for g in range(2):
                    column[i][g] = column[i][g] - weight[g] * other
            for value, kept in zip(rows, factor):
                other = jnp.broadcast_to(value[h][q : q + 1, :], (8, 128))
                kept[h] = jnp.where(sublane == q, other, kept[h])
                for g in range(2):
                    value[g] = value[g] - weight[g] * other
            if j in (3, 9) and work:
                work.pop(0)()
        scale = [lax.rsqrt(value) for value in pivots]
        for s, kept in enumerate(factor):
            ref, at_rows, columns = at(s, here)
            ref[at_rows, columns] = jnp.concatenate([kept[g] * scale[g] for g in range(2)], axis=0)
        if p < panels - 1:
            solved = jnp.concatenate(
                [
                    jnp.concatenate([value[g] * inverses[g] for g in range(2)], axis=0)
                    for value in rows
                ],
                axis=1,
            )
            right = right_parts(solved, 0)
            right = jnp.concatenate([right, jnp.zeros((128 - 6 * PANEL, right.shape[1]), BF16)], axis=0)
            parts_ref[:, : (width + 1) * 128] = right
            after = slice(first + PANEL, first + 2 * PANEL)
            lose(after, column_parts(a_ref[after, tile(t)], p * PANEL, None), right)
    while work:
        work.pop(0)()


def whiten_kernel(
    scale, gram_ref, smooth_ref, scores_ref, a_ref, w_ref, parts_ref, wp_ref, up_ref, left_ref, scores, load_sem, out_sems
):
    load = pltpu.make_async_copy(smooth_ref, left_ref, load_sem)
    load.start()
    for n, (i, j) in enumerate(BLOCKS):
        a_ref[tile(i), tile(j)] = gram_ref[tile(n), :]
    size = left_ref.shape[0] // PIECES
    copies = []

    def solve(t, n):
        here = slice(n * size, (n + 1) * size)
        value = lax.dot_general(
            left_parts(left_ref[here, tile(t)], 1),
            wp_ref[t],
            (((1,), (1,)), ((), ())),
            preferred_element_type=F32,
        )
        scores[here, tile(t)] = value * scale
        if t < 3:
            behind = (3 - t) * 128
            left_ref[here, (t + 1) * 128 :] -= dot(left_parts(value, 1), up_ref[t, :, :behind])
        copy = pltpu.make_async_copy(
            scores.at[here, tile(t)], scores_ref.at[here, tile(t)], out_sems.at[t, n]
        )
        copy.start()
        copies.append(copy)

    row = lax.broadcasted_iota(jnp.int32, (128, 128), 0)
    lane = lax.broadcasted_iota(jnp.int32, (128, 128), 1)
    identity = jnp.where(row == lane, 1.0, 0.0).astype(F32)
    work = []
    for t in range(4):
        w_ref[tile(t), :] = identity
        factor_block(t, a_ref, w_ref, parts_ref, work)
        if t == 0:
            load.wait()
        wp_ref[t] = right_parts(w_ref[tile(t), :], 1)
        if t < 3:
            behind = (3 - t) * 128
            up_ref[t, :, :behind] = right_parts(a_ref[tile(t), (t + 1) * 128 :], 0)

            def trail(s, t=t):
                a_ref[tile(s), s * 128 :] -= dot(
                    left_parts(a_ref[tile(t), tile(s)].T, 1),
                    up_ref[t, :, (s - t - 1) * 128 : (3 - t) * 128],
                )

            trail(t + 1)
            work += [functools.partial(trail, s) for s in range(t + 2, 4)]
        work += [functools.partial(solve, t, n) for n in range(PIECES)]
    while work:
        work.pop(0)()
    for copy in copies:
        copy.wait()


def whiten_call(gram, smooth, scale):
    rows = smooth.shape[0]

    def kernel(*refs):
        whiten_kernel(scale, *refs)

    return pl.pallas_call(
        kernel,
        out_shape=jax.ShapeDtypeStruct((rows, BINS), F32),
        in_specs=[
            pl.BlockSpec(memory_space=pltpu.VMEM),
            pl.BlockSpec(memory_space=pl.ANY),
        ],
        out_specs=pl.BlockSpec(memory_space=pl.ANY),
        scratch_shapes=[
            pltpu.VMEM((BINS, BINS), F32),
            pltpu.VMEM((BINS, 128), F32),
            pltpu.VMEM((128, 5 * 128), BF16),
            pltpu.VMEM((4, 128, 6 * 128), BF16),
            pltpu.VMEM((3, 6 * 128, 3 * 128), BF16),
            pltpu.VMEM((rows, BINS), F32),
            pltpu.VMEM((rows, BINS), F32),
            pltpu.SemaphoreType.DMA,
            pltpu.SemaphoreType.DMA((4, PIECES)),
        ],
        compiler_params=pltpu.CompilerParams(vmem_limit_bytes=62 << 20),
    )(gram, smooth)


def local(counts, spread):
    gram, smooth = gram_call(counts, spread.reshape(1, BINS))
    rows_all = smooth.shape[0] * lax.axis_size("gx") * lax.axis_size("gy")
    scores = whiten_call(gram, smooth, math.sqrt(rows_all))
    return scores.reshape(counts.shape)


def solution(mesh):
    in_specs = (P(None, "gx", "gy", None), P())
    out_specs = P(None, "gx", "gy", None)
    return jax.shard_map(local, mesh=mesh, in_specs=in_specs, out_specs=out_specs, check_vma=False)
```

```python
import functools
import math

import jax
import jax.numpy as jnp
from jax import lax
from jax.experimental import pallas as pl
from jax.experimental.pallas import tpu as pltpu
from jax.sharding import PartitionSpec as P

RADIUS = 2
BINS = 512
PLANES = 4
SIDE = 16
CORES = 2
X_CHIPS = 4
Y_CHIPS = 8
Z_CHIPS = 8
F32 = jnp.float32
BF16 = jnp.bfloat16
MESH = pl.DeviceIdType.MESH

BLOCKS = [(i, j) for i in range(4) for j in range(i, 4)]
PACKED = len(BLOCKS) * 128
CHUNKS = [(0, 512), (512, PACKED - 512)]


def shares(rows):
    half = rows // CORES
    quarter = half // X_CHIPS
    eighth = -(-quarter // (8 * Z_CHIPS)) * 8
    return half, quarter, eighth


PANEL = 16
PIECES = 8


def split3(x):
    high = x.astype(BF16)
    rest = x - high.astype(F32)
    middle = rest.astype(BF16)
    return high, middle, (rest - middle.astype(F32)).astype(BF16)


def left_parts(x, axis):
    high, middle, low = split3(x)
    return jnp.concatenate([high, high, middle, high, low, middle], axis=axis)


def right_parts(x, axis):
    high, middle, low = split3(x)
    return jnp.concatenate([high, middle, high, low, high, middle], axis=axis)


def tile(s):
    return slice(s * 128, s * 128 + 128)


def dot(left, right):
    return jnp.dot(left, right, preferred_element_type=F32)


def tap_rows(spread):
    offsets = [float(k) for k in range(-RADIUS, RADIUS + 1)]
    profile = [jnp.exp(-k * k / (2.0 * spread * spread)) for k in offsets]
    total = profile[0]
    for row in profile[1:]:
        total = total + row
    return [row / total for row in profile]


def gram_kernel(
    counts_ref,
    spread_ref,
    gram_ref,
    smooth_ref,
    grid,
    blurred,
    smooth,
    edge_out,
    edge_in,
    corner_out,
    corner_in,
    packed,
    from_core0,
    from_x0,
    quarter0,
    from_z0,
    from_y0,
    gathered0,
    from_core1,
    from_x1,
    quarter1,
    from_z1,
    from_y1,
    gathered1,
    whole,
    taps_in,
    load_sems,
    taps_sem,
    x_send,
    x_recv,
    y_send,
    y_recv,
    c_send,
    c_recv,
    red_send,
    red_recv,
    out_sems,
):
    gx, gy = lax.axis_index("gx"), lax.axis_index("gy")
    nx, ny = CORES * Y_CHIPS, Z_CHIPS * X_CHIPS
    core, y = lax.rem(gx, CORES), gx // CORES
    x, z = lax.rem(gy, X_CHIPS), gy // X_CHIPS

    taps_load = pltpu.make_async_copy(spread_ref, taps_in, taps_sem)
    taps_load.start()
    loads = []
    for p in range(PLANES):
        load = pltpu.make_async_copy(
            counts_ref.at[p],
            grid.at[p, RADIUS : RADIUS + SIDE, 8 : 8 + SIDE, :],
            load_sems.at[p],
        )
        load.start()
        loads.append(load)

    def core_peer():
        return (y * CORES + 1 - core, gy)

    def x_peer(d):
        return (gx, z * X_CHIPS + lax.rem(x + d, X_CHIPS))

    def z_peer(d):
        return (gx, lax.rem(z + d, Z_CHIPS) * X_CHIPS + x)

    def y_peer(d):
        return (lax.rem(y + d, Y_CHIPS) * CORES + core, gy)

    def beside(dx, dy):
        return (lax.rem(gx + dx + nx, nx), lax.rem(gy + dy + ny, ny))

    around = [(dx, dy) for dx in (-1, 0, 1) for dy in (-1, 0, 1) if (dx, dy) != (0, 0)]
    partners = [beside(dx, dy) for dx, dy in around]
    partners += [core_peer()]
    partners += [x_peer(d) for d in range(1, X_CHIPS)]
    partners += [z_peer(d) for d in range(1, Z_CHIPS)]
    partners += [y_peer(d) for d in range(1, Y_CHIPS)]
    barrier = pltpu.get_barrier_semaphore()
    for partner in partners:
        pl.semaphore_signal(barrier, inc=1, device_id=partner, device_id_type=MESH)

    def there(dx, dy):
        inside = None
        for delta, here, size in ((dx, gx, nx), (dy, gy, ny)):
            if delta:
                test = here > 0 if delta < 0 else here < size - 1
                inside = test if inside is None else jnp.logical_and(inside, test)
        return inside

    for p in range(PLANES):
        loads[p].wait()
        for i in range(SIDE):
            row = grid[p, RADIUS + i, 8:16, :]
            edge_out[0, p, 2 * i : 2 * i + 2, :] = row[0:2]
            row2 = grid[p, RADIUS + i, 16:24, :]
            edge_out[1, p, 2 * i : 2 * i + 2, :] = row2[6:8]
        for a, first in ((0, 0), (1, SIDE - 2)):
            for b in (0, 1):
                corner_out[2 * a + b, 4 * p : 4 * p + 4, :] = edge_out[
                    b, p, 2 * first : 2 * first + 4, :
                ]

    pl.semaphore_wait(barrier, len(partners))

    def x_copy(p, side):
        rows = (RADIUS, RADIUS + SIDE - 2)[side]
        lands = (RADIUS + SIDE, 0)[side]
        return pltpu.make_async_remote_copy(
            src_ref=grid.at[p, rows : rows + 2, 8 : 8 + SIDE, :],
            dst_ref=grid.at[p, lands : lands + 2, 8 : 8 + SIDE, :],
            send_sem=x_send.at[p, side],
            recv_sem=x_recv.at[p, side],
            device_id=beside((-1, 1)[side], 0),
            device_id_type=MESH,
        )

    def y_copy(p, side):
        return pltpu.make_async_remote_copy(
            src_ref=edge_out.at[side, p],
            dst_ref=edge_in.at[1 - side, p],
            send_sem=y_send.at[p, side],
            recv_sem=y_recv.at[p, side],
            device_id=beside(0, (-1, 1)[side]),
            device_id_type=MESH,
        )

    def corner_copy(a, b):
        return pltpu.make_async_remote_copy(
            src_ref=corner_out.at[2 * a + b],
            dst_ref=corner_in.at[2 * (1 - a) + 1 - b],
            send_sem=c_send.at[2 * a + b],
            recv_sem=c_recv.at[2 * a + b],
            device_id=beside((-1, 1)[a], (-1, 1)[b]),
            device_id_type=MESH,
        )

    sign = (-1, 1)
    for a in (0, 1):
        for b in (0, 1):

            @pl.when(there(sign[a], sign[b]))
            def _():
                corner_copy(a, b).start()

            @pl.when(jnp.logical_not(there(sign[a], sign[b])))
            def _():
                corner_in[2 * a + b] = jnp.zeros((4 * PLANES, BINS), F32)

    for p in range(PLANES):
        for side in (0, 1):

            @pl.when(there(0, sign[side]))
            def _():
                y_copy(p, side).start()

            @pl.when(there(sign[side], 0))
            def _():
                x_copy(p, side).start()

    for side in (0, 1):

        @pl.when(jnp.logical_not(there(0, sign[side])))
        def _():
            edge_in[side] = jnp.zeros((PLANES, 2 * SIDE, BINS), F32)

        @pl.when(jnp.logical_not(there(sign[side], 0)))
        def _():
            lands = (0, RADIUS + SIDE)[side]
            for p in range(PLANES):
                grid[p, lands : lands + 2, 8 : 8 + SIDE, :] = jnp.zeros((2, SIDE, BINS), F32)

    taps_load.wait()
    taps = tap_rows(taps_in[...])

    for a in (0, 1):
        for b in (0, 1):

            @pl.when(there(sign[1 - a], sign[1 - b]))
            def _():
                corner_copy(a, b).wait_recv()

    def rows_at(start, size):
        return pl.ds(pl.multiple_of(start, 8), size)

    buffers = [
        (from_core0, from_x0, quarter0, from_z0, from_y0, gathered0),
        (from_core1, from_x1, quarter1, from_z1, from_y1, gathered1),
    ]
    leaves = []
    gives = []

    def reduction(c):
        first, rows = CHUNKS[c]
        half, fourth, eighth = shares(rows)
        from_core, from_x, quarter, from_z, from_y, gathered = buffers[c]

        def send(step, source, target, device):
            pltpu.make_async_remote_copy(
                src_ref=source,
                dst_ref=target,
                send_sem=red_send.at[c, step],
                recv_sem=red_recv.at[c, step],
                device_id=device,
                device_id_type=MESH,
            ).start()

        def arrived(step, landed):
            pltpu.make_async_copy(landed, landed, red_recv.at[c, step]).wait()

        def left(step, gone):
            leaves.append(lambda: pltpu.make_async_copy(gone, gone, red_send.at[c, step]).wait())

        send(0, packed.at[rows_at(first + (1 - core) * half, half)], from_core, core_peer())
        left(0, from_core)
        if fourth < Z_CHIPS * eighth:
            quarter[fourth:, :] = jnp.zeros((Z_CHIPS * eighth - fourth, 128), F32)
        yield
        arrived(0, from_core)
        mine = first + core * half
        packed[rows_at(mine, half), :] += from_core[...]

        for d in range(1, X_CHIPS):
            send(
                1,
                packed.at[rows_at(mine + lax.rem(x + d, X_CHIPS) * fourth, fourth)],
                from_x.at[d - 1],
                x_peer(d),
            )
        left(1, from_x)
        yield
        arrived(1, from_x)
        total = packed[rows_at(mine + x * fourth, fourth), :]
        for d in range(X_CHIPS - 1):
            total = total + from_x[d]
        quarter[0:fourth, :] = total

        for d in (4, 3, 5, 2, 6, 1, 7):
            send(
                2,
                quarter.at[rows_at(lax.rem(z + d, Z_CHIPS) * eighth, eighth)],
                from_z.at[d - 1],
                z_peer(d),
            )
        left(2, from_z)
        yield
        arrived(2, from_z)
        total = quarter[rows_at(z * eighth, eighth), :]
        for d in range(Z_CHIPS - 1):
            total = total + from_z[d]

        from_y[y] = total
        for d in (4, 3, 5, 2, 6, 1, 7):
            send(3, from_y.at[y], from_y.at[y], y_peer(d))
        left(3, from_y.at[1:])
        yield
        arrived(3, from_y.at[1:])
        total = from_y[0]
        for d in range(1, Y_CHIPS):
            total = total + from_y[d]

        here = rows_at(z * eighth, eighth)
        gathered[here, :] = total
        for d in (4, 3, 5, 2, 6, 1, 7):
            send(4, gathered.at[here], gathered.at[here], z_peer(d))
        left(4, gathered.at[eighth:])
        yield
        arrived(4, gathered.at[eighth:])
        here = rows_at(mine + x * fourth, fourth)
        for d in range(1, X_CHIPS):
            send(5, gathered.at[0:fourth], whole.at[here], x_peer(d))
        left(5, from_x)
        whole[here, :] = gathered[0:fourth, :]
        yield
        arrived(5, from_x)
        here = rows_at(mine, half)
        send(6, whole.at[here], whole.at[here], core_peer())
        left(6, from_core)
        yield
        arrived(6, from_core)
        give = pltpu.make_async_copy(
            whole.at[first : first + rows], gram_ref.at[first : first + rows], out_sems.at[PLANES + c]
        )
        give.start()
        gives.append(give)

    keeps = []
    for p in range(PLANES):
        for side in (0, 1):

            @pl.when(there(0, sign[1 - side]))
            def _():
                y_copy(p, side).wait_recv()

            @pl.when(there(sign[1 - side], 0))
            def _():
                x_copy(p, side).wait_recv()

        for b, lands in ((0, 6), (1, 8 + SIDE)):
            for i in range(SIDE):
                grid[p, RADIUS + i, lands : lands + 2, :] = edge_in[b, p, 2 * i : 2 * i + 2, :]
            for a, first in ((0, 0), (1, RADIUS + SIDE)):
                for i in (0, 1):
                    grid[p, first + i, lands : lands + 2, :] = corner_in[
                        2 * a + b, 4 * p + 2 * i : 4 * p + 2 * i + 2, :
                    ]

        def along_x(i, carry, p=p):
            for lo, hi in ((0, 8), (8, 24), (24, 32)):
                total = taps[0] * grid[p, i, lo:hi, :]
                for k in range(1, 2 * RADIUS + 1):
                    total = total + taps[k] * grid[p, i + k, lo:hi, :]
                blurred[i, lo:hi, :] = total
            return carry

        lax.fori_loop(0, SIDE, along_x, 0)

        def along_y(i, carry, p=p):
            total = taps[0] * blurred[i, 6 : 6 + SIDE, :]
            for k in range(1, 2 * RADIUS + 1):
                total = total + taps[k] * blurred[i, 6 + k : 6 + k + SIDE, :]
            at = pl.multiple_of(p * SIDE * SIDE + i * SIDE, SIDE)
            smooth[pl.ds(at, SIDE), :] = total
            return carry

        lax.fori_loop(0, SIDE, along_y, 0)
        rows = slice(p * SIDE * SIDE, (p + 1) * SIDE * SIDE)
        keep = pltpu.make_async_copy(smooth.at[rows], smooth_ref.at[rows], out_sems.at[p])
        keep.start()
        keeps.append(keep)

        value = smooth[rows, :]
        high, middle, _ = split3(value.T)
        left = jnp.concatenate([high, high, middle, middle], axis=1)
        high, middle, _ = split3(value)
        right = jnp.concatenate([high, middle, high, middle], axis=0)
        at = 0
        for i in range(4):
            part = dot(left[tile(i), :], right[:, i * 128 :])
            for j in range(4 - i):
                block = part[:, tile(j)]
                if p == 0:
                    packed[at : at + 128, :] = block
                else:
                    packed[at : at + 128, :] += block
                at += 128
            if p == PLANES - 1 and i == 0:
                first_chunk = reduction(0)
                next(first_chunk)

    second_chunk = reduction(1)
    next(second_chunk)
    for p in range(PLANES):
        for side in (0, 1):

            @pl.when(there(0, sign[side]))
            def _():
                y_copy(p, side).wait_send()

            @pl.when(there(sign[side], 0))
            def _():
                x_copy(p, side).wait_send()

        keeps[p].wait()
    for a in (0, 1):
        for b in (0, 1):

            @pl.when(there(sign[a], sign[b]))
            def _():
                corner_copy(a, b).wait_send()

    under_way = [first_chunk, second_chunk]
    while under_way:
        under_way = [chunk for chunk in under_way if next(chunk, chunk) is not chunk]
    for wait in leaves:
        wait()
    for give in gives:
        give.wait()


def gram_call(counts, spread):
    dma = pltpu.SemaphoreType.DMA
    rows = PLANES * SIDE * SIDE
    reduction_buffers = []
    for _, chunk in CHUNKS:
        half, fourth, eighth = shares(chunk)
        for shape in (
            (half,),
            (X_CHIPS - 1, fourth),
            (Z_CHIPS * eighth,),
            (Z_CHIPS - 1, eighth),
            (Y_CHIPS, eighth),
            (Z_CHIPS * eighth,),
        ):
            reduction_buffers.append(pltpu.VMEM((*shape, 128), F32))
    return pl.pallas_call(
        gram_kernel,
        out_shape=[
            jax.ShapeDtypeStruct((PACKED, 128), F32),
            jax.ShapeDtypeStruct((rows, BINS), F32),
        ],
        in_specs=[pl.BlockSpec(memory_space=pl.ANY)] * 2,
        out_specs=[pl.BlockSpec(memory_space=pl.ANY)] * 2,
        scratch_shapes=[
            pltpu.VMEM((PLANES, SIDE + 2 * RADIUS, SIDE + 16, BINS), F32),
            pltpu.VMEM((SIDE, SIDE + 16, BINS), F32),
            pltpu.VMEM((rows, BINS), F32),
            pltpu.VMEM((2, PLANES, 2 * SIDE, BINS), F32),
            pltpu.VMEM((2, PLANES, 2 * SIDE, BINS), F32),
            pltpu.VMEM((4, 4 * PLANES, BINS), F32),
            pltpu.VMEM((4, 4 * PLANES, BINS), F32),
            pltpu.VMEM((PACKED, 128), F32),
            *reduction_buffers,
            pltpu.VMEM((PACKED, 128), F32),
            pltpu.VMEM((1, BINS), F32),
            dma((PLANES,)),
            dma,
            dma((PLANES, 2)),
            dma((PLANES, 2)),
            dma((PLANES, 2)),
            dma((PLANES, 2)),
            dma((4,)),
            dma((4,)),
            dma((2, 7)),
            dma((2, 7)),
            dma((PLANES + 2,)),
        ],
        compiler_params=pltpu.CompilerParams(
            collective_id=0, has_side_effects=True, vmem_limit_bytes=62 << 20
        ),
    )(counts, spread)


def factor_block(t, a_ref, w_ref, parts_ref, work):
    sublane = lax.broadcasted_iota(jnp.int32, (8, 128), 0)
    panels = 128 // PANEL
    width = 4 - t

    def at(s, rows):
        return (a_ref, rows, tile(t + s)) if s < width else (w_ref, rows, slice(0, 128))

    def column_parts(value, first, keep):
        lane = lax.broadcasted_iota(jnp.int32, value.shape, 1)
        column = jnp.take_along_axis(value, first + lane % PANEL, axis=1)
        if keep is not None:
            column = jnp.where(keep, column, 0.0)
        high, middle, low = split3(column)
        high, middle, low = high.astype(F32), middle.astype(F32), low.astype(F32)
        group = lane // PANEL
        value = jnp.where(
            (group == 0) | (group == 1) | (group == 3),
            high,
            jnp.where((group == 2) | (group == 5), middle, jnp.where(group == 4, low, 0.0)),
        )
        return value.astype(BF16)

    def lose(rows, left, right, skip=0):
        update = dot(left, right[:, skip * 128 :])
        for s in range(skip, width + 1):
            ref, at_rows, columns = at(s, rows)
            ref[at_rows, columns] -= update[:, tile(s - skip)]

    for p in range(panels):
        first = t * 128 + p * PANEL
        here = slice(first, first + PANEL)
        rows = []
        for s in range(width + 1):
            ref, at_rows, columns = at(s, here)
            rows.append([ref[first + 8 * g : first + 8 * g + 8, columns] for g in range(2)])
        column = [
            [
                jnp.take_along_axis(
                    rows[0][g], jnp.full((8, 128), p * PANEL + j, jnp.int32), axis=1
                )
                for g in range(2)
            ]
            for j in range(PANEL)
        ]
        factor = [list(value) for value in rows]
        pivots = [jnp.ones((8, 128), F32)] * 2
        inverses = [jnp.ones((8, 128), F32)] * 2
        if 0 < p < panels - 1:
            beyond = slice(first + PANEL, t * 128 + 128)
            left = column_parts(a_ref[beyond, tile(t)], (p - 1) * PANEL, None)
            lose(beyond, left, parts_ref[:, : (width + 1) * 128])
        if p < panels - 1:
            after = slice(first + PANEL, first + 2 * PANEL)
            below = [a_ref[first + PANEL + 8 * g : first + PANEL + 8 * g + 8, tile(t)] for g in range(2)]
        under = []
        for j in range(PANEL):
            h, q = divmod(j, 8)
            pivot = jnp.broadcast_to(column[j][h][q : q + 1, :], (8, 128))
            inverse = 1.0 / pivot
            pivots[h] = jnp.where(sublane == q, pivot, pivots[h])
            inverses[h] = jnp.where(sublane == q, inverse, inverses[h])
            if p < panels - 1:
                at_lane = jnp.full((8, 128), p * PANEL + j, jnp.int32)
                under.append([jnp.take_along_axis(value, at_lane, axis=1) * inverse for value in below])
            weight = [
                (jnp.where(sublane != q, column[j][g], 0.0) if g == h else column[j][g]) * inverse
                for g in range(2)
            ]
            for i in range(j + 1, PANEL):
                other = jnp.broadcast_to(column[i][h][q : q + 1, :], (8, 128))
                for g in range(2):
                    column[i][g] = column[i][g] - weight[g] * other
            for value, kept in zip(rows, factor):
                other = jnp.broadcast_to(value[h][q : q + 1, :], (8, 128))
                kept[h] = jnp.where(sublane == q, other, kept[h])
                for g in range(2):
                    value[g] = value[g] - weight[g] * other
            if (j == 6 or (j == 12 and p < 2)) and work:
                work.pop(0)()
        scale = [lax.rsqrt(value) for value in pivots]
        for s, kept in enumerate(factor):
            ref, at_rows, columns = at(s, here)
            ref[at_rows, columns] = jnp.concatenate([kept[g] * scale[g] for g in range(2)], axis=0)
        if p < panels - 1:
            solved = jnp.concatenate(
                [
                    jnp.concatenate([value[g] * inverses[g] for g in range(2)], axis=0)
                    for value in rows
                ],
                axis=1,
            )
            right = right_parts(solved, 0)
            right = jnp.concatenate([right, jnp.zeros((128 - 6 * PANEL, right.shape[1]), BF16)], axis=0)
            parts_ref[:, : (width + 1) * 128] = right
            for g in range(2):
                sums = [below[g], None]
                for j in range(PANEL):
                    other = jnp.broadcast_to(rows[0][j // 8][j % 8 : j % 8 + 1, :], (8, 128))
                    term = under[j][g] * other
                    k = j % 2
                    sums[k] = -term if sums[k] is None else sums[k] - term
                low_rows = slice(first + PANEL + 8 * g, first + PANEL + 8 * g + 8)
                a_ref[low_rows, tile(t)] = sums[0] + sums[1]
            lose(after, column_parts(jnp.concatenate(below, axis=0), p * PANEL, None), right, 1)
    while work:
        work.pop(0)()


def whiten_kernel(
    scale, gram_ref, smooth_ref, scores_ref, a_ref, w_ref, parts_ref, wp_ref, up_ref, left_ref, scores, load_sem, out_sems
):
    load = pltpu.make_async_copy(smooth_ref, left_ref, load_sem)
    load.start()
    for n, (i, j) in enumerate(BLOCKS):
        a_ref[tile(i), tile(j)] = gram_ref[tile(n), :]
    size = left_ref.shape[0] // PIECES
    copies = []

    def solve(t, n):
        here = slice(n * size, (n + 1) * size)
        value = lax.dot_general(
            left_parts(left_ref[here, tile(t)], 1),
            wp_ref[t],
            (((1,), (1,)), ((), ())),
            preferred_element_type=F32,
        )
        scores[here, tile(t)] = value * scale
        if t < 3:
            behind = (3 - t) * 128
            left_ref[here, (t + 1) * 128 :] -= dot(left_parts(value, 1), up_ref[t, :, :behind])
        copy = pltpu.make_async_copy(
            scores.at[here, tile(t)], scores_ref.at[here, tile(t)], out_sems.at[t, n]
        )
        copy.start()
        copies.append(copy)

    row = lax.broadcasted_iota(jnp.int32, (128, 128), 0)
    lane = lax.broadcasted_iota(jnp.int32, (128, 128), 1)
    identity = jnp.where(row == lane, 1.0, 0.0).astype(F32)
    work = []
    for t in range(4):
        w_ref[tile(t), :] = identity
        factor_block(t, a_ref, w_ref, parts_ref, work)
        if t == 0:
            load.wait()
        wp_ref[t] = right_parts(w_ref[tile(t), :], 1)
        if t < 3:
            behind = (3 - t) * 128
            up_ref[t, :, :behind] = right_parts(a_ref[tile(t), (t + 1) * 128 :], 0)

            def trail(s, t=t):
                a_ref[tile(s), s * 128 :] -= dot(
                    left_parts(a_ref[tile(t), tile(s)].T, 1),
                    up_ref[t, :, (s - t - 1) * 128 : (3 - t) * 128],
                )

            trail(t + 1)
            work += [functools.partial(trail, s) for s in range(t + 2, 4)]
        work += [functools.partial(solve, t, n) for n in range(PIECES)]
    while work:
        work.pop(0)()
    for copy in copies:
        copy.wait()


def whiten_call(gram, smooth, scale):
    rows = smooth.shape[0]

    def kernel(*refs):
        whiten_kernel(scale, *refs)

    return pl.pallas_call(
        kernel,
        out_shape=jax.ShapeDtypeStruct((rows, BINS), F32),
        in_specs=[
            pl.BlockSpec(memory_space=pltpu.VMEM),
            pl.BlockSpec(memory_space=pl.ANY),
        ],
        out_specs=pl.BlockSpec(memory_space=pl.ANY),
        scratch_shapes=[
            pltpu.VMEM((BINS, BINS), F32),
            pltpu.VMEM((BINS, 128), F32),
            pltpu.VMEM((128, 5 * 128), BF16),
            pltpu.VMEM((4, 128, 6 * 128), BF16),
            pltpu.VMEM((3, 6 * 128, 3 * 128), BF16),
            pltpu.VMEM((rows, BINS), F32),
            pltpu.VMEM((rows, BINS), F32),
            pltpu.SemaphoreType.DMA,
            pltpu.SemaphoreType.DMA((4, PIECES)),
        ],
        compiler_params=pltpu.CompilerParams(vmem_limit_bytes=62 << 20),
    )(gram, smooth)


def local(counts, spread):
    gram, smooth = gram_call(counts, spread.reshape(1, BINS))
    rows_all = smooth.shape[0] * lax.axis_size("gx") * lax.axis_size("gy")
    scores = whiten_call(gram, smooth, math.sqrt(rows_all))
    return scores.reshape(counts.shape)


def solution(mesh):
    in_specs = (P(None, "gx", "gy", None), P())
    out_specs = P(None, "gx", "gy", None)
    return jax.shard_map(local, mesh=mesh, in_specs=in_specs, out_specs=out_specs, check_vma=False)
```

```python
import functools
import math

import jax
import jax.numpy as jnp
from jax import lax
from jax.experimental import pallas as pl
from jax.experimental.pallas import tpu as pltpu
from jax.sharding import PartitionSpec as P

RADIUS = 2
BINS = 512
PLANES = 4
SIDE = 16
CORES = 2
X_CHIPS = 4
Y_CHIPS = 8
Z_CHIPS = 8
F32 = jnp.float32
BF16 = jnp.bfloat16
MESH = pl.DeviceIdType.MESH

BLOCKS = [(i, j) for i in range(4) for j in range(i, 4)]
PACKED = len(BLOCKS) * 128
CHUNKS = [(0, 512), (512, PACKED - 512)]


def shares(rows):
    half = rows // CORES
    quarter = half // X_CHIPS
    eighth = -(-quarter // (8 * Z_CHIPS)) * 8
    return half, quarter, eighth


PANEL = 16
PIECES = 8


def split3(x):
    high = x.astype(BF16)
    rest = x - high.astype(F32)
    middle = rest.astype(BF16)
    return high, middle, (rest - middle.astype(F32)).astype(BF16)


def left_parts(x, axis):
    high, middle, low = split3(x)
    return jnp.concatenate([high, high, middle, high, low, middle], axis=axis)


def right_parts(x, axis):
    high, middle, low = split3(x)
    return jnp.concatenate([high, middle, high, low, high, middle], axis=axis)


def tile(s):
    return slice(s * 128, s * 128 + 128)


def dot(left, right):
    return jnp.dot(left, right, preferred_element_type=F32)


def tap_rows(spread):
    offsets = [float(k) for k in range(-RADIUS, RADIUS + 1)]
    profile = [jnp.exp(-k * k / (2.0 * spread * spread)) for k in offsets]
    total = profile[0]
    for row in profile[1:]:
        total = total + row
    return [row / total for row in profile]


def gram_kernel(
    counts_ref,
    spread_ref,
    gram_ref,
    smooth_ref,
    grid,
    blurred,
    smooth,
    edge_out,
    edge_in,
    corner_out,
    corner_in,
    packed,
    from_core0,
    from_x0,
    quarter0,
    from_z0,
    from_y0,
    gathered0,
    from_core1,
    from_x1,
    quarter1,
    from_z1,
    from_y1,
    gathered1,
    whole,
    taps_in,
    load_sems,
    taps_sem,
    x_send,
    x_recv,
    y_send,
    y_recv,
    c_send,
    c_recv,
    red_send,
    red_recv,
    out_sems,
):
    gx, gy = lax.axis_index("gx"), lax.axis_index("gy")
    nx, ny = CORES * Y_CHIPS, Z_CHIPS * X_CHIPS
    core, y = lax.rem(gx, CORES), gx // CORES
    x, z = lax.rem(gy, X_CHIPS), gy // X_CHIPS

    taps_load = pltpu.make_async_copy(spread_ref, taps_in, taps_sem)
    taps_load.start()
    loads = []
    for p in range(PLANES):
        load = pltpu.make_async_copy(
            counts_ref.at[p],
            grid.at[p, RADIUS : RADIUS + SIDE, 8 : 8 + SIDE, :],
            load_sems.at[p],
        )
        load.start()
        loads.append(load)

    def core_peer():
        return (y * CORES + 1 - core, gy)

    def x_peer(d):
        return (gx, z * X_CHIPS + lax.rem(x + d, X_CHIPS))

    def z_peer(d):
        return (gx, lax.rem(z + d, Z_CHIPS) * X_CHIPS + x)

    def y_peer(d):
        return (lax.rem(y + d, Y_CHIPS) * CORES + core, gy)

    def beside(dx, dy):
        return (lax.rem(gx + dx + nx, nx), lax.rem(gy + dy + ny, ny))

    around = [(dx, dy) for dx in (-1, 0, 1) for dy in (-1, 0, 1) if (dx, dy) != (0, 0)]
    partners = [beside(dx, dy) for dx, dy in around]
    partners += [core_peer()]
    partners += [x_peer(d) for d in range(1, X_CHIPS)]
    partners += [z_peer(d) for d in range(1, Z_CHIPS)]
    partners += [y_peer(d) for d in range(1, Y_CHIPS)]
    barrier = pltpu.get_barrier_semaphore()
    for partner in partners:
        pl.semaphore_signal(barrier, inc=1, device_id=partner, device_id_type=MESH)

    def there(dx, dy):
        inside = None
        for delta, here, size in ((dx, gx, nx), (dy, gy, ny)):
            if delta:
                test = here > 0 if delta < 0 else here < size - 1
                inside = test if inside is None else jnp.logical_and(inside, test)
        return inside

    for p in range(PLANES):
        loads[p].wait()
        for i in range(SIDE):
            row = grid[p, RADIUS + i, 8:16, :]
            edge_out[0, p, 2 * i : 2 * i + 2, :] = row[0:2]
            row2 = grid[p, RADIUS + i, 16:24, :]
            edge_out[1, p, 2 * i : 2 * i + 2, :] = row2[6:8]
        for a, first in ((0, 0), (1, SIDE - 2)):
            for b in (0, 1):
                corner_out[2 * a + b, 4 * p : 4 * p + 4, :] = edge_out[
                    b, p, 2 * first : 2 * first + 4, :
                ]

    pl.semaphore_wait(barrier, len(partners))

    def x_copy(p, side):
        rows = (RADIUS, RADIUS + SIDE - 2)[side]
        lands = (RADIUS + SIDE, 0)[side]
        return pltpu.make_async_remote_copy(
            src_ref=grid.at[p, rows : rows + 2, 8 : 8 + SIDE, :],
            dst_ref=grid.at[p, lands : lands + 2, 8 : 8 + SIDE, :],
            send_sem=x_send.at[p, side],
            recv_sem=x_recv.at[p, side],
            device_id=beside((-1, 1)[side], 0),
            device_id_type=MESH,
        )

    def y_copy(p, side):
        return pltpu.make_async_remote_copy(
            src_ref=edge_out.at[side, p],
            dst_ref=edge_in.at[1 - side, p],
            send_sem=y_send.at[p, side],
            recv_sem=y_recv.at[p, side],
            device_id=beside(0, (-1, 1)[side]),
            device_id_type=MESH,
        )

    def corner_copy(a, b):
        return pltpu.make_async_remote_copy(
            src_ref=corner_out.at[2 * a + b],
            dst_ref=corner_in.at[2 * (1 - a) + 1 - b],
            send_sem=c_send.at[2 * a + b],
            recv_sem=c_recv.at[2 * a + b],
            device_id=beside((-1, 1)[a], (-1, 1)[b]),
            device_id_type=MESH,
        )

    sign = (-1, 1)
    for a in (0, 1):
        for b in (0, 1):

            @pl.when(there(sign[a], sign[b]))
            def _():
                corner_copy(a, b).start()

            @pl.when(jnp.logical_not(there(sign[a], sign[b])))
            def _():
                corner_in[2 * a + b] = jnp.zeros((4 * PLANES, BINS), F32)

    for p in range(PLANES):
        for side in (0, 1):

            @pl.when(there(0, sign[side]))
            def _():
                y_copy(p, side).start()

            @pl.when(there(sign[side], 0))
            def _():
                x_copy(p, side).start()

    for side in (0, 1):

        @pl.when(jnp.logical_not(there(0, sign[side])))
        def _():
            edge_in[side] = jnp.zeros((PLANES, 2 * SIDE, BINS), F32)

        @pl.when(jnp.logical_not(there(sign[side], 0)))
        def _():
            lands = (0, RADIUS + SIDE)[side]
            for p in range(PLANES):
                grid[p, lands : lands + 2, 8 : 8 + SIDE, :] = jnp.zeros((2, SIDE, BINS), F32)

    taps_load.wait()
    taps = tap_rows(taps_in[...])

    def along_x(p, i, lo, hi):
        total = taps[0] * grid[p, i, lo:hi, :]
        for k in range(1, 2 * RADIUS + 1):
            total = total + taps[k] * grid[p, i + k, lo:hi, :]
        blurred[p, i, lo:hi, :] = total

    for p in range(PLANES):

        def inner_x(i, carry, p=p):
            along_x(p, i, 8, 8 + SIDE)
            return carry

        lax.fori_loop(RADIUS, SIDE - RADIUS, inner_x, 0)

    for a in (0, 1):
        for b in (0, 1):

            @pl.when(there(sign[1 - a], sign[1 - b]))
            def _():
                corner_copy(a, b).wait_recv()

    def rows_at(start, size):
        return pl.ds(pl.multiple_of(start, 8), size)

    buffers = [
        (from_core0, from_x0, quarter0, from_z0, from_y0, gathered0),
        (from_core1, from_x1, quarter1, from_z1, from_y1, gathered1),
    ]
    leaves = []
    gives = []

    def reduction(c):
        first, rows = CHUNKS[c]
        half, fourth, eighth = shares(rows)
        from_core, from_x, quarter, from_z, from_y, gathered = buffers[c]

        def send(step, source, target, device):
            pltpu.make_async_remote_copy(
                src_ref=source,
                dst_ref=target,
                send_sem=red_send.at[c, step],
                recv_sem=red_recv.at[c, step],
                device_id=device,
                device_id_type=MESH,
            ).start()

        def arrived(step, landed):
            pltpu.make_async_copy(landed, landed, red_recv.at[c, step]).wait()

        def left(step, gone):
            leaves.append(lambda: pltpu.make_async_copy(gone, gone, red_send.at[c, step]).wait())

        send(0, packed.at[rows_at(first + (1 - core) * half, half)], from_core, core_peer())
        left(0, from_core)
        if fourth < Z_CHIPS * eighth:
            quarter[fourth:, :] = jnp.zeros((Z_CHIPS * eighth - fourth, 128), F32)
        yield
        arrived(0, from_core)
        mine = first + core * half
        packed[rows_at(mine, half), :] += from_core[...]

        for d in range(1, X_CHIPS):
            send(
                1,
                packed.at[rows_at(mine + lax.rem(x + d, X_CHIPS) * fourth, fourth)],
                from_x.at[d - 1],
                x_peer(d),
            )
        left(1, from_x)
        yield
        arrived(1, from_x)
        total = packed[rows_at(mine + x * fourth, fourth), :]
        for d in range(X_CHIPS - 1):
            total = total + from_x[d]
        quarter[0:fourth, :] = total

        for d in (4, 3, 5, 2, 6, 1, 7):
            send(
                2,
                quarter.at[rows_at(lax.rem(z + d, Z_CHIPS) * eighth, eighth)],
                from_z.at[d - 1],
                z_peer(d),
            )
        left(2, from_z)
        yield
        arrived(2, from_z)
        total = quarter[rows_at(z * eighth, eighth), :]
        for d in range(Z_CHIPS - 1):
            total = total + from_z[d]

        from_y[y] = total
        for d in (4, 3, 5, 2, 6, 1, 7):
            send(3, from_y.at[y], from_y.at[y], y_peer(d))
        left(3, from_y.at[1:])
        yield
        arrived(3, from_y.at[1:])
        total = from_y[0]
        for d in range(1, Y_CHIPS):
            total = total + from_y[d]

        here = rows_at(z * eighth, eighth)
        gathered[here, :] = total
        for d in (4, 3, 5, 2, 6, 1, 7):
            send(4, gathered.at[here], gathered.at[here], z_peer(d))
        left(4, gathered.at[eighth:])
        yield
        arrived(4, gathered.at[eighth:])
        here = rows_at(mine + x * fourth, fourth)
        for d in range(1, X_CHIPS):
            send(5, gathered.at[0:fourth], whole.at[here], x_peer(d))
        left(5, from_x)
        whole[here, :] = gathered[0:fourth, :]
        yield
        arrived(5, from_x)
        here = rows_at(mine, half)
        send(6, whole.at[here], whole.at[here], core_peer())
        left(6, from_core)
        yield
        arrived(6, from_core)
        give = pltpu.make_async_copy(
            whole.at[first : first + rows], gram_ref.at[first : first + rows], out_sems.at[PLANES + c]
        )
        give.start()
        gives.append(give)

    keeps = []
    for p in range(PLANES):
        for side in (0, 1):

            @pl.when(there(0, sign[1 - side]))
            def _():
                y_copy(p, side).wait_recv()

            @pl.when(there(sign[1 - side], 0))
            def _():
                x_copy(p, side).wait_recv()

        for b, lands in ((0, 6), (1, 8 + SIDE)):
            for i in range(SIDE):
                grid[p, RADIUS + i, lands : lands + 2, :] = edge_in[b, p, 2 * i : 2 * i + 2, :]
            for a, first in ((0, 0), (1, RADIUS + SIDE)):
                for i in (0, 1):
                    grid[p, first + i, lands : lands + 2, :] = corner_in[
                        2 * a + b, 4 * p + 2 * i : 4 * p + 2 * i + 2, :
                    ]

        def beside_x(i, carry, p=p):
            along_x(p, i, 0, 8)
            along_x(p, i, 8 + SIDE, 16 + SIDE)
            return carry

        lax.fori_loop(0, SIDE, beside_x, 0)
        for i in (0, 1, SIDE - 2, SIDE - 1):
            along_x(p, i, 8, 8 + SIDE)

        def along_y(i, carry, p=p):
            total = taps[0] * blurred[p, i, 6 : 6 + SIDE, :]
            for k in range(1, 2 * RADIUS + 1):
                total = total + taps[k] * blurred[p, i, 6 + k : 6 + k + SIDE, :]
            at = pl.multiple_of(p * SIDE * SIDE + i * SIDE, SIDE)
            smooth[pl.ds(at, SIDE), :] = total
            return carry

        lax.fori_loop(0, SIDE, along_y, 0)
        rows = slice(p * SIDE * SIDE, (p + 1) * SIDE * SIDE)
        keep = pltpu.make_async_copy(smooth.at[rows], smooth_ref.at[rows], out_sems.at[p])
        keep.start()
        keeps.append(keep)

        value = smooth[rows, :]
        high, middle, _ = split3(value.T)
        left = jnp.concatenate([high, high, middle, middle], axis=1)
        high, middle, _ = split3(value)
        right = jnp.concatenate([high, middle, high, middle], axis=0)
        at = 0
        for i in range(4):
            part = dot(left[tile(i), :], right[:, i * 128 :])
            for j in range(4 - i):
                block = part[:, tile(j)]
                if p == 0:
                    packed[at : at + 128, :] = block
                else:
                    packed[at : at + 128, :] += block
                at += 128
            if p == PLANES - 1 and i == 0:
                first_chunk = reduction(0)
                next(first_chunk)

    second_chunk = reduction(1)
    next(second_chunk)
    for p in range(PLANES):
        for side in (0, 1):

            @pl.when(there(0, sign[side]))
            def _():
                y_copy(p, side).wait_send()

            @pl.when(there(sign[side], 0))
            def _():
                x_copy(p, side).wait_send()

        keeps[p].wait()
    for a in (0, 1):
        for b in (0, 1):

            @pl.when(there(sign[a], sign[b]))
            def _():
                corner_copy(a, b).wait_send()

    under_way = [first_chunk, second_chunk]
    while under_way:
        under_way = [chunk for chunk in under_way if next(chunk, chunk) is not chunk]
    for wait in leaves:
        wait()
    for give in gives:
        give.wait()


def gram_call(counts, spread):
    dma = pltpu.SemaphoreType.DMA
    rows = PLANES * SIDE * SIDE
    reduction_buffers = []
    for _, chunk in CHUNKS:
        half, fourth, eighth = shares(chunk)
        for shape in (
            (half,),
            (X_CHIPS - 1, fourth),
            (Z_CHIPS * eighth,),
            (Z_CHIPS - 1, eighth),
            (Y_CHIPS, eighth),
            (Z_CHIPS * eighth,),
        ):
            reduction_buffers.append(pltpu.VMEM((*shape, 128), F32))
    return pl.pallas_call(
        gram_kernel,
        out_shape=[
            jax.ShapeDtypeStruct((PACKED, 128), F32),
            jax.ShapeDtypeStruct((rows, BINS), F32),
        ],
        in_specs=[pl.BlockSpec(memory_space=pl.ANY)] * 2,
        out_specs=[pl.BlockSpec(memory_space=pl.ANY)] * 2,
        scratch_shapes=[
            pltpu.VMEM((PLANES, SIDE + 2 * RADIUS, SIDE + 16, BINS), F32),
            pltpu.VMEM((PLANES, SIDE, SIDE + 16, BINS), F32),
            pltpu.VMEM((rows, BINS), F32),
            pltpu.VMEM((2, PLANES, 2 * SIDE, BINS), F32),
            pltpu.VMEM((2, PLANES, 2 * SIDE, BINS), F32),
            pltpu.VMEM((4, 4 * PLANES, BINS), F32),
            pltpu.VMEM((4, 4 * PLANES, BINS), F32),
            pltpu.VMEM((PACKED, 128), F32),
            *reduction_buffers,
            pltpu.VMEM((PACKED, 128), F32),
            pltpu.VMEM((1, BINS), F32),
            dma((PLANES,)),
            dma,
            dma((PLANES, 2)),
            dma((PLANES, 2)),
            dma((PLANES, 2)),
            dma((PLANES, 2)),
            dma((4,)),
            dma((4,)),
            dma((2, 7)),
            dma((2, 7)),
            dma((PLANES + 2,)),
        ],
        compiler_params=pltpu.CompilerParams(
            collective_id=0, has_side_effects=True, vmem_limit_bytes=62 << 20
        ),
    )(counts, spread)


def factor_block(t, a_ref, w_ref, parts_ref, work):
    sublane = lax.broadcasted_iota(jnp.int32, (8, 128), 0)
    panels = 128 // PANEL
    width = 4 - t

    def at(s, rows):
        return (a_ref, rows, tile(t + s)) if s < width else (w_ref, rows, slice(0, 128))

    def column_parts(value, first, keep):
        lane = lax.broadcasted_iota(jnp.int32, value.shape, 1)
        column = jnp.take_along_axis(value, first + lane % PANEL, axis=1)
        if keep is not None:
            column = jnp.where(keep, column, 0.0)
        high, middle, low = split3(column)
        high, middle, low = high.astype(F32), middle.astype(F32), low.astype(F32)
        group = lane // PANEL
        value = jnp.where(
            (group == 0) | (group == 1) | (group == 3),
            high,
            jnp.where((group == 2) | (group == 5), middle, jnp.where(group == 4, low, 0.0)),
        )
        return value.astype(BF16)

    def lose(rows, left, right, skip=0):
        update = dot(left, right[:, skip * 128 :])
        for s in range(skip, width + 1):
            ref, at_rows, columns = at(s, rows)
            ref[at_rows, columns] -= update[:, tile(s - skip)]

    for p in range(panels):
        first = t * 128 + p * PANEL
        here = slice(first, first + PANEL)
        rows = []
        for s in range(width + 1):
            ref, at_rows, columns = at(s, here)
            rows.append([ref[first + 8 * g : first + 8 * g + 8, columns] for g in range(2)])
        column = [
            [
                jnp.take_along_axis(
                    rows[0][g], jnp.full((8, 128), p * PANEL + j, jnp.int32), axis=1
                )
                for g in range(2)
            ]
            for j in range(PANEL)
        ]
        factor = [list(value) for value in rows]
        pivots = [jnp.ones((8, 128), F32)] * 2
        inverses = [jnp.ones((8, 128), F32)] * 2
        if 0 < p < panels - 1:
            beyond = slice(first + PANEL, t * 128 + 128)
            left = column_parts(a_ref[beyond, tile(t)], (p - 1) * PANEL, None)
            lose(beyond, left, parts_ref[:, : (width + 1) * 128])
        if p < panels - 1:
            after = slice(first + PANEL, first + 2 * PANEL)
            below = [a_ref[first + PANEL + 8 * g : first + PANEL + 8 * g + 8, tile(t)] for g in range(2)]
        under = []
        for j in range(PANEL):
            h, q = divmod(j, 8)
            pivot = jnp.broadcast_to(column[j][h][q : q + 1, :], (8, 128))
            inverse = 1.0 / pivot
            pivots[h] = jnp.where(sublane == q, pivot, pivots[h])
            inverses[h] = jnp.where(sublane == q, inverse, inverses[h])
            if p < panels - 1:
                at_lane = jnp.full((8, 128), p * PANEL + j, jnp.int32)
                under.append([jnp.take_along_axis(value, at_lane, axis=1) * inverse for value in below])
            weight = [
                (jnp.where(sublane != q, column[j][g], 0.0) if g == h else column[j][g]) * inverse
                for g in range(2)
            ]
            for i in range(j + 1, PANEL):
                other = jnp.broadcast_to(column[i][h][q : q + 1, :], (8, 128))
                for g in range(2):
                    column[i][g] = column[i][g] - weight[g] * other
            for value, kept in zip(rows, factor):
                other = jnp.broadcast_to(value[h][q : q + 1, :], (8, 128))
                kept[h] = jnp.where(sublane == q, other, kept[h])
                for g in range(2):
                    value[g] = value[g] - weight[g] * other
            if (j == 6 or (j == 12 and p < 2)) and work:
                work.pop(0)()
        scale = [lax.rsqrt(value) for value in pivots]
        for s, kept in enumerate(factor):
            ref, at_rows, columns = at(s, here)
            ref[at_rows, columns] = jnp.concatenate([kept[g] * scale[g] for g in range(2)], axis=0)
        if p < panels - 1:
            solved = jnp.concatenate(
                [
                    jnp.concatenate([value[g] * inverses[g] for g in range(2)], axis=0)
                    for value in rows
                ],
                axis=1,
            )
            right = right_parts(solved, 0)
            right = jnp.concatenate([right, jnp.zeros((128 - 6 * PANEL, right.shape[1]), BF16)], axis=0)
            parts_ref[:, : (width + 1) * 128] = right
            for g in range(2):
                sums = [below[g], None]
                for j in range(PANEL):
                    other = jnp.broadcast_to(rows[0][j // 8][j % 8 : j % 8 + 1, :], (8, 128))
                    term = under[j][g] * other
                    k = j % 2
                    sums[k] = -term if sums[k] is None else sums[k] - term
                low_rows = slice(first + PANEL + 8 * g, first + PANEL + 8 * g + 8)
                a_ref[low_rows, tile(t)] = sums[0] + sums[1]
            lose(after, column_parts(jnp.concatenate(below, axis=0), p * PANEL, None), right, 1)
    while work:
        work.pop(0)()


def whiten_kernel(
    scale, gram_ref, smooth_ref, scores_ref, a_ref, w_ref, parts_ref, wp_ref, up_ref, left_ref, scores, load_sem, out_sems
):
    load = pltpu.make_async_copy(smooth_ref, left_ref, load_sem)
    load.start()
    for n, (i, j) in enumerate(BLOCKS):
        a_ref[tile(i), tile(j)] = gram_ref[tile(n), :]
    size = left_ref.shape[0] // PIECES
    copies = []

    def solve(t, n):
        here = slice(n * size, (n + 1) * size)
        value = lax.dot_general(
            left_parts(left_ref[here, tile(t)], 1),
            wp_ref[t],
            (((1,), (1,)), ((), ())),
            preferred_element_type=F32,
        )
        scores[here, tile(t)] = value * scale
        if t < 3:
            behind = (3 - t) * 128
            left_ref[here, (t + 1) * 128 :] -= dot(left_parts(value, 1), up_ref[t, :, :behind])
        copy = pltpu.make_async_copy(
            scores.at[here, tile(t)], scores_ref.at[here, tile(t)], out_sems.at[t, n]
        )
        copy.start()
        copies.append(copy)

    row = lax.broadcasted_iota(jnp.int32, (128, 128), 0)
    lane = lax.broadcasted_iota(jnp.int32, (128, 128), 1)
    identity = jnp.where(row == lane, 1.0, 0.0).astype(F32)
    work = []
    for t in range(4):
        w_ref[tile(t), :] = identity
        factor_block(t, a_ref, w_ref, parts_ref, work)
        if t == 0:
            load.wait()
        wp_ref[t] = right_parts(w_ref[tile(t), :], 1)
        if t < 3:
            behind = (3 - t) * 128
            up_ref[t, :, :behind] = right_parts(a_ref[tile(t), (t + 1) * 128 :], 0)

            def trail(s, t=t):
                a_ref[tile(s), s * 128 :] -= dot(
                    left_parts(a_ref[tile(t), tile(s)].T, 1),
                    up_ref[t, :, (s - t - 1) * 128 : (3 - t) * 128],
                )

            trail(t + 1)
            work += [functools.partial(trail, s) for s in range(t + 2, 4)]
        work += [functools.partial(solve, t, n) for n in range(PIECES)]
    while work:
        work.pop(0)()
    for copy in copies:
        copy.wait()


def whiten_call(gram, smooth, scale):
    rows = smooth.shape[0]

    def kernel(*refs):
        whiten_kernel(scale, *refs)

    return pl.pallas_call(
        kernel,
        out_shape=jax.ShapeDtypeStruct((rows, BINS), F32),
        in_specs=[
            pl.BlockSpec(memory_space=pltpu.VMEM),
            pl.BlockSpec(memory_space=pl.ANY),
        ],
        out_specs=pl.BlockSpec(memory_space=pl.ANY),
        scratch_shapes=[
            pltpu.VMEM((BINS, BINS), F32),
            pltpu.VMEM((BINS, 128), F32),
            pltpu.VMEM((128, 5 * 128), BF16),
            pltpu.VMEM((4, 128, 6 * 128), BF16),
            pltpu.VMEM((3, 6 * 128, 3 * 128), BF16),
            pltpu.VMEM((rows, BINS), F32),
            pltpu.VMEM((rows, BINS), F32),
            pltpu.SemaphoreType.DMA,
            pltpu.SemaphoreType.DMA((4, PIECES)),
        ],
        compiler_params=pltpu.CompilerParams(vmem_limit_bytes=62 << 20),
    )(gram, smooth)


def local(counts, spread):
    gram, smooth = gram_call(counts, spread.reshape(1, BINS))
    rows_all = smooth.shape[0] * lax.axis_size("gx") * lax.axis_size("gy")
    scores = whiten_call(gram, smooth, math.sqrt(rows_all))
    return scores.reshape(counts.shape)


def solution(mesh):
    in_specs = (P(None, "gx", "gy", None), P())
    out_specs = P(None, "gx", "gy", None)
    return jax.shard_map(local, mesh=mesh, in_specs=in_specs, out_specs=out_specs, check_vma=False)
```

```python
import functools
import math

import jax
import jax.numpy as jnp
from jax import lax
from jax.experimental import pallas as pl
from jax.experimental.pallas import tpu as pltpu
from jax.sharding import PartitionSpec as P

RADIUS = 2
BINS = 512
PLANES = 4
SIDE = 16
CORES = 2
X_CHIPS = 4
Y_CHIPS = 8
Z_CHIPS = 8
F32 = jnp.float32
BF16 = jnp.bfloat16
MESH = pl.DeviceIdType.MESH

BLOCKS = [(i, j) for i in range(4) for j in range(i, 4)]
PACKED = len(BLOCKS) * 128
CHUNKS = [(0, 512), (512, PACKED - 512)]


def shares(rows):
    half = rows // CORES
    quarter = half // X_CHIPS
    eighth = -(-quarter // (8 * Z_CHIPS)) * 8
    return half, quarter, eighth


PANEL = 16
PIECES = 8


def split3(x):
    high = x.astype(BF16)
    rest = x - high.astype(F32)
    middle = rest.astype(BF16)
    return high, middle, (rest - middle.astype(F32)).astype(BF16)


def left_parts(x, axis):
    high, middle, low = split3(x)
    return jnp.concatenate([high, high, middle, high, low, middle], axis=axis)


def right_parts(x, axis):
    high, middle, low = split3(x)
    return jnp.concatenate([high, middle, high, low, high, middle], axis=axis)


def tile(s):
    return slice(s * 128, s * 128 + 128)


def dot(left, right):
    return jnp.dot(left, right, preferred_element_type=F32)


def tap_rows(spread):
    offsets = [float(k) for k in range(-RADIUS, RADIUS + 1)]
    profile = [jnp.exp(-k * k / (2.0 * spread * spread)) for k in offsets]
    total = profile[0]
    for row in profile[1:]:
        total = total + row
    return [row / total for row in profile]


def gram_kernel(
    counts_ref,
    spread_ref,
    gram_ref,
    smooth_ref,
    grid,
    blurred,
    smooth,
    edge_out,
    edge_in,
    corner_out,
    corner_in,
    packed,
    from_core0,
    from_x0,
    quarter0,
    from_z0,
    from_y0,
    gathered0,
    from_core1,
    from_x1,
    quarter1,
    from_z1,
    from_y1,
    gathered1,
    whole,
    taps_in,
    load_sems,
    taps_sem,
    x_send,
    x_recv,
    y_send,
    y_recv,
    c_send,
    c_recv,
    red_send,
    red_recv,
    out_sems,
):
    gx, gy = lax.axis_index("gx"), lax.axis_index("gy")
    nx, ny = CORES * Y_CHIPS, Z_CHIPS * X_CHIPS
    core, y = lax.rem(gx, CORES), gx // CORES
    x, z = lax.rem(gy, X_CHIPS), gy // X_CHIPS

    taps_load = pltpu.make_async_copy(spread_ref, taps_in, taps_sem)
    taps_load.start()
    loads = []
    for p in range(PLANES):
        load = pltpu.make_async_copy(
            counts_ref.at[p],
            grid.at[p, RADIUS : RADIUS + SIDE, 8 : 8 + SIDE, :],
            load_sems.at[p],
        )
        load.start()
        loads.append(load)

    def core_peer():
        return (y * CORES + 1 - core, gy)

    def x_peer(d):
        return (gx, z * X_CHIPS + lax.rem(x + d, X_CHIPS))

    def z_peer(d):
        return (gx, lax.rem(z + d, Z_CHIPS) * X_CHIPS + x)

    def y_peer(d):
        return (lax.rem(y + d, Y_CHIPS) * CORES + core, gy)

    def beside(dx, dy):
        return (lax.rem(gx + dx + nx, nx), lax.rem(gy + dy + ny, ny))

    around = [(dx, dy) for dx in (-1, 0, 1) for dy in (-1, 0, 1) if (dx, dy) != (0, 0)]
    partners = [beside(dx, dy) for dx, dy in around]
    partners += [core_peer()]
    partners += [x_peer(d) for d in range(1, X_CHIPS)]
    partners += [z_peer(d) for d in range(1, Z_CHIPS)]
    partners += [y_peer(d) for d in range(1, Y_CHIPS)]
    barrier = pltpu.get_barrier_semaphore()
    for partner in partners:
        pl.semaphore_signal(barrier, inc=1, device_id=partner, device_id_type=MESH)

    def there(dx, dy):
        inside = None
        for delta, here, size in ((dx, gx, nx), (dy, gy, ny)):
            if delta:
                test = here > 0 if delta < 0 else here < size - 1
                inside = test if inside is None else jnp.logical_and(inside, test)
        return inside

    for p in range(PLANES):
        loads[p].wait()
        for i in range(SIDE):
            row = grid[p, RADIUS + i, 8:16, :]
            edge_out[0, p, 2 * i : 2 * i + 2, :] = row[0:2]
            row2 = grid[p, RADIUS + i, 16:24, :]
            edge_out[1, p, 2 * i : 2 * i + 2, :] = row2[6:8]
        for a, first in ((0, 0), (1, SIDE - 2)):
            for b in (0, 1):
                corner_out[2 * a + b, 4 * p : 4 * p + 4, :] = edge_out[
                    b, p, 2 * first : 2 * first + 4, :
                ]

    pl.semaphore_wait(barrier, len(partners))

    def x_copy(p, side):
        rows = (RADIUS, RADIUS + SIDE - 2)[side]
        lands = (RADIUS + SIDE, 0)[side]
        return pltpu.make_async_remote_copy(
            src_ref=grid.at[p, rows : rows + 2, 8 : 8 + SIDE, :],
            dst_ref=grid.at[p, lands : lands + 2, 8 : 8 + SIDE, :],
            send_sem=x_send.at[p, side],
            recv_sem=x_recv.at[p, side],
            device_id=beside((-1, 1)[side], 0),
            device_id_type=MESH,
        )

    def y_copy(p, side):
        return pltpu.make_async_remote_copy(
            src_ref=edge_out.at[side, p],
            dst_ref=edge_in.at[1 - side, p],
            send_sem=y_send.at[p, side],
            recv_sem=y_recv.at[p, side],
            device_id=beside(0, (-1, 1)[side]),
            device_id_type=MESH,
        )

    def corner_copy(a, b):
        return pltpu.make_async_remote_copy(
            src_ref=corner_out.at[2 * a + b],
            dst_ref=corner_in.at[2 * (1 - a) + 1 - b],
            send_sem=c_send.at[2 * a + b],
            recv_sem=c_recv.at[2 * a + b],
            device_id=beside((-1, 1)[a], (-1, 1)[b]),
            device_id_type=MESH,
        )

    sign = (-1, 1)
    for a in (0, 1):
        for b in (0, 1):

            @pl.when(there(sign[a], sign[b]))
            def _():
                corner_copy(a, b).start()

            @pl.when(jnp.logical_not(there(sign[a], sign[b])))
            def _():
                corner_in[2 * a + b] = jnp.zeros((4 * PLANES, BINS), F32)

    for p in range(PLANES):
        for side in (0, 1):

            @pl.when(there(0, sign[side]))
            def _():
                y_copy(p, side).start()

            @pl.when(there(sign[side], 0))
            def _():
                x_copy(p, side).start()

    for side in (0, 1):

        @pl.when(jnp.logical_not(there(0, sign[side])))
        def _():
            edge_in[side] = jnp.zeros((PLANES, 2 * SIDE, BINS), F32)

        @pl.when(jnp.logical_not(there(sign[side], 0)))
        def _():
            lands = (0, RADIUS + SIDE)[side]
            for p in range(PLANES):
                grid[p, lands : lands + 2, 8 : 8 + SIDE, :] = jnp.zeros((2, SIDE, BINS), F32)

    taps_load.wait()
    taps = tap_rows(taps_in[...])

    def along_x(p, i, lo, hi):
        total = taps[0] * grid[p, i, lo:hi, :]
        for k in range(1, 2 * RADIUS + 1):
            total = total + taps[k] * grid[p, i + k, lo:hi, :]
        blurred[p, i, lo:hi, :] = total

    for p in range(PLANES):

        def inner_x(i, carry, p=p):
            along_x(p, i, 8, 8 + SIDE)
            return carry

        lax.fori_loop(RADIUS, SIDE - RADIUS, inner_x, 0)

    for a in (0, 1):
        for b in (0, 1):

            @pl.when(there(sign[1 - a], sign[1 - b]))
            def _():
                corner_copy(a, b).wait_recv()

    def rows_at(start, size):
        return pl.ds(pl.multiple_of(start, 8), size)

    buffers = [
        (from_core0, from_x0, quarter0, from_z0, from_y0, gathered0),
        (from_core1, from_x1, quarter1, from_z1, from_y1, gathered1),
    ]
    leaves = []
    gives = []

    def reduction(c):
        first, rows = CHUNKS[c]
        half, fourth, eighth = shares(rows)
        from_core, from_x, quarter, from_z, from_y, gathered = buffers[c]

        def send(step, source, target, device):
            pltpu.make_async_remote_copy(
                src_ref=source,
                dst_ref=target,
                send_sem=red_send.at[c, step],
                recv_sem=red_recv.at[c, step],
                device_id=device,
                device_id_type=MESH,
            ).start()

        def arrived(step, landed):
            pltpu.make_async_copy(landed, landed, red_recv.at[c, step]).wait()

        def left(step, gone):
            leaves.append(lambda: pltpu.make_async_copy(gone, gone, red_send.at[c, step]).wait())

        send(0, packed.at[rows_at(first + (1 - core) * half, half)], from_core, core_peer())
        left(0, from_core)
        if fourth < Z_CHIPS * eighth:
            quarter[fourth:, :] = jnp.zeros((Z_CHIPS * eighth - fourth, 128), F32)
        yield
        arrived(0, from_core)
        mine = first + core * half
        packed[rows_at(mine, half), :] += from_core[...]

        for d in range(1, X_CHIPS):
            send(
                1,
                packed.at[rows_at(mine + lax.rem(x + d, X_CHIPS) * fourth, fourth)],
                from_x.at[d - 1],
                x_peer(d),
            )
        left(1, from_x)
        yield
        arrived(1, from_x)
        total = packed[rows_at(mine + x * fourth, fourth), :]
        for d in range(X_CHIPS - 1):
            total = total + from_x[d]
        quarter[0:fourth, :] = total

        for d in (4, 3, 5, 2, 6, 1, 7):
            send(
                2,
                quarter.at[rows_at(lax.rem(z + d, Z_CHIPS) * eighth, eighth)],
                from_z.at[d - 1],
                z_peer(d),
            )
        left(2, from_z)
        yield
        arrived(2, from_z)
        total = quarter[rows_at(z * eighth, eighth), :]
        for d in range(Z_CHIPS - 1):
            total = total + from_z[d]

        from_y[y] = total
        for d in (4, 3, 5, 2, 6, 1, 7):
            send(3, from_y.at[y], from_y.at[y], y_peer(d))
        left(3, from_y.at[1:])
        yield
        arrived(3, from_y.at[1:])
        total = from_y[0]
        for d in range(1, Y_CHIPS):
            total = total + from_y[d]

        here = rows_at(z * eighth, eighth)
        gathered[here, :] = total
        for d in (4, 3, 5, 2, 6, 1, 7):
            send(4, gathered.at[here], gathered.at[here], z_peer(d))
        left(4, gathered.at[eighth:])
        yield
        arrived(4, gathered.at[eighth:])
        here = rows_at(mine + x * fourth, fourth)
        for d in range(1, X_CHIPS):
            send(5, gathered.at[0:fourth], whole.at[here], x_peer(d))
        left(5, from_x)
        whole[here, :] = gathered[0:fourth, :]
        yield
        arrived(5, from_x)
        here = rows_at(mine, half)
        send(6, whole.at[here], whole.at[here], core_peer())
        left(6, from_core)
        yield
        arrived(6, from_core)
        give = pltpu.make_async_copy(
            whole.at[first : first + rows], gram_ref.at[first : first + rows], out_sems.at[PLANES + c]
        )
        give.start()
        gives.append(give)

    squares = jnp.zeros((1, BINS), F32)
    diagonal = lax.broadcasted_iota(jnp.int32, (128, 128), 0) == lax.broadcasted_iota(
        jnp.int32, (128, 128), 1
    )
    keeps = []
    for p in range(PLANES):
        for side in (0, 1):

            @pl.when(there(0, sign[1 - side]))
            def _():
                y_copy(p, side).wait_recv()

            @pl.when(there(sign[1 - side], 0))
            def _():
                x_copy(p, side).wait_recv()

        for b, lands in ((0, 6), (1, 8 + SIDE)):
            for i in range(SIDE):
                grid[p, RADIUS + i, lands : lands + 2, :] = edge_in[b, p, 2 * i : 2 * i + 2, :]
            for a, first in ((0, 0), (1, RADIUS + SIDE)):
                for i in (0, 1):
                    grid[p, first + i, lands : lands + 2, :] = corner_in[
                        2 * a + b, 4 * p + 2 * i : 4 * p + 2 * i + 2, :
                    ]

        def beside_x(i, carry, p=p):
            along_x(p, i, 0, 8)
            along_x(p, i, 8 + SIDE, 16 + SIDE)
            return carry

        lax.fori_loop(0, SIDE, beside_x, 0)
        for i in (0, 1, SIDE - 2, SIDE - 1):
            along_x(p, i, 8, 8 + SIDE)

        def along_y(i, carry, p=p):
            total = taps[0] * blurred[p, i, 6 : 6 + SIDE, :]
            for k in range(1, 2 * RADIUS + 1):
                total = total + taps[k] * blurred[p, i, 6 + k : 6 + k + SIDE, :]
            at = pl.multiple_of(p * SIDE * SIDE + i * SIDE, SIDE)
            smooth[pl.ds(at, SIDE), :] = total
            return carry

        lax.fori_loop(0, SIDE, along_y, 0)
        rows = slice(p * SIDE * SIDE, (p + 1) * SIDE * SIDE)
        keep = pltpu.make_async_copy(smooth.at[rows], smooth_ref.at[rows], out_sems.at[p])
        keep.start()
        keeps.append(keep)

        value = smooth[rows, :]
        high, middle, _ = split3(value.T)
        left = jnp.concatenate([high, high, middle], axis=1)
        high, middle, _ = split3(value)
        right = jnp.concatenate([high, middle, high], axis=0)
        middle = middle.astype(F32)
        squares = squares + jnp.sum(middle * middle, axis=0, keepdims=True)
        at = 0
        for i in range(4):
            part = dot(left[tile(i), :], right[:, i * 128 :])
            for j in range(4 - i):
                block = part[:, tile(j)]
                if p == PLANES - 1 and j == 0:
                    block = block + jnp.where(diagonal, squares[:, tile(i)], 0.0)
                if p == 0:
                    packed[at : at + 128, :] = block
                else:
                    packed[at : at + 128, :] += block
                at += 128
            if p == PLANES - 1 and i == 0:
                first_chunk = reduction(0)
                next(first_chunk)

    second_chunk = reduction(1)
    next(second_chunk)
    for p in range(PLANES):
        for side in (0, 1):

            @pl.when(there(0, sign[side]))
            def _():
                y_copy(p, side).wait_send()

            @pl.when(there(sign[side], 0))
            def _():
                x_copy(p, side).wait_send()

        keeps[p].wait()
    for a in (0, 1):
        for b in (0, 1):

            @pl.when(there(sign[a], sign[b]))
            def _():
                corner_copy(a, b).wait_send()

    under_way = [first_chunk, second_chunk]
    while under_way:
        under_way = [chunk for chunk in under_way if next(chunk, chunk) is not chunk]
    for wait in leaves:
        wait()
    for give in gives:
        give.wait()


def gram_call(counts, spread):
    dma = pltpu.SemaphoreType.DMA
    rows = PLANES * SIDE * SIDE
    reduction_buffers = []
    for _, chunk in CHUNKS:
        half, fourth, eighth = shares(chunk)
        for shape in (
            (half,),
            (X_CHIPS - 1, fourth),
            (Z_CHIPS * eighth,),
            (Z_CHIPS - 1, eighth),
            (Y_CHIPS, eighth),
            (Z_CHIPS * eighth,),
        ):
            reduction_buffers.append(pltpu.VMEM((*shape, 128), F32))
    return pl.pallas_call(
        gram_kernel,
        out_shape=[
            jax.ShapeDtypeStruct((PACKED, 128), F32),
            jax.ShapeDtypeStruct((rows, BINS), F32),
        ],
        in_specs=[pl.BlockSpec(memory_space=pl.ANY)] * 2,
        out_specs=[pl.BlockSpec(memory_space=pl.ANY)] * 2,
        scratch_shapes=[
            pltpu.VMEM((PLANES, SIDE + 2 * RADIUS, SIDE + 16, BINS), F32),
            pltpu.VMEM((PLANES, SIDE, SIDE + 16, BINS), F32),
            pltpu.VMEM((rows, BINS), F32),
            pltpu.VMEM((2, PLANES, 2 * SIDE, BINS), F32),
            pltpu.VMEM((2, PLANES, 2 * SIDE, BINS), F32),
            pltpu.VMEM((4, 4 * PLANES, BINS), F32),
            pltpu.VMEM((4, 4 * PLANES, BINS), F32),
            pltpu.VMEM((PACKED, 128), F32),
            *reduction_buffers,
            pltpu.VMEM((PACKED, 128), F32),
            pltpu.VMEM((1, BINS), F32),
            dma((PLANES,)),
            dma,
            dma((PLANES, 2)),
            dma((PLANES, 2)),
            dma((PLANES, 2)),
            dma((PLANES, 2)),
            dma((4,)),
            dma((4,)),
            dma((2, 7)),
            dma((2, 7)),
            dma((PLANES + 2,)),
        ],
        compiler_params=pltpu.CompilerParams(
            collective_id=0, has_side_effects=True, vmem_limit_bytes=62 << 20
        ),
    )(counts, spread)


def factor_block(t, a_ref, w_ref, parts_ref, work):
    sublane = lax.broadcasted_iota(jnp.int32, (8, 128), 0)
    panels = 128 // PANEL
    width = 4 - t

    def at(s, rows):
        return (a_ref, rows, tile(t + s)) if s < width else (w_ref, rows, slice(0, 128))

    def column_parts(value, first, keep):
        lane = lax.broadcasted_iota(jnp.int32, value.shape, 1)
        column = jnp.take_along_axis(value, first + lane % PANEL, axis=1)
        if keep is not None:
            column = jnp.where(keep, column, 0.0)
        high, middle, low = split3(column)
        high, middle, low = high.astype(F32), middle.astype(F32), low.astype(F32)
        group = lane // PANEL
        value = jnp.where(
            (group == 0) | (group == 1) | (group == 3),
            high,
            jnp.where((group == 2) | (group == 5), middle, jnp.where(group == 4, low, 0.0)),
        )
        return value.astype(BF16)

    def lose(rows, left, right, skip=0):
        update = dot(left, right[:, skip * 128 :])
        for s in range(skip, width + 1):
            ref, at_rows, columns = at(s, rows)
            ref[at_rows, columns] -= update[:, tile(s - skip)]

    for p in range(panels):
        first = t * 128 + p * PANEL
        here = slice(first, first + PANEL)
        rows = []
        for s in range(width + 1):
            ref, at_rows, columns = at(s, here)
            rows.append([ref[first + 8 * g : first + 8 * g + 8, columns] for g in range(2)])
        column = [
            [
                jnp.take_along_axis(
                    rows[0][g], jnp.full((8, 128), p * PANEL + j, jnp.int32), axis=1
                )
                for g in range(2)
            ]
            for j in range(PANEL)
        ]
        factor = [list(value) for value in rows]
        pivots = [jnp.ones((8, 128), F32)] * 2
        inverses = [jnp.ones((8, 128), F32)] * 2
        if 0 < p < panels - 1:
            beyond = slice(first + PANEL, t * 128 + 128)
            left = column_parts(a_ref[beyond, tile(t)], (p - 1) * PANEL, None)
            lose(beyond, left, parts_ref[:, : (width + 1) * 128])
        if p < panels - 1:
            after = slice(first + PANEL, first + 2 * PANEL)
            below = [a_ref[first + PANEL + 8 * g : first + PANEL + 8 * g + 8, tile(t)] for g in range(2)]
        under = []
        for j in range(PANEL):
            h, q = divmod(j, 8)
            pivot = jnp.broadcast_to(column[j][h][q : q + 1, :], (8, 128))
            inverse = 1.0 / pivot
            pivots[h] = jnp.where(sublane == q, pivot, pivots[h])
            inverses[h] = jnp.where(sublane == q, inverse, inverses[h])
            if p < panels - 1:
                at_lane = jnp.full((8, 128), p * PANEL + j, jnp.int32)
                under.append([jnp.take_along_axis(value, at_lane, axis=1) * inverse for value in below])
            weight = [
                (jnp.where(sublane != q, column[j][g], 0.0) if g == h else column[j][g]) * inverse
                for g in range(2)
            ]
            for i in range(j + 1, PANEL):
                other = jnp.broadcast_to(column[i][h][q : q + 1, :], (8, 128))
                for g in range(2):
                    column[i][g] = column[i][g] - weight[g] * other
            for value, kept in zip(rows, factor):
                other = jnp.broadcast_to(value[h][q : q + 1, :], (8, 128))
                kept[h] = jnp.where(sublane == q, other, kept[h])
                for g in range(2):
                    value[g] = value[g] - weight[g] * other
            if (j == 6 or (j == 12 and p < 2)) and work:
                work.pop(0)()
        scale = [lax.rsqrt(value) for value in pivots]
        for s, kept in enumerate(factor):
            ref, at_rows, columns = at(s, here)
            ref[at_rows, columns] = jnp.concatenate([kept[g] * scale[g] for g in range(2)], axis=0)
        if p < panels - 1:
            solved = jnp.concatenate(
                [
                    jnp.concatenate([value[g] * inverses[g] for g in range(2)], axis=0)
                    for value in rows
                ],
                axis=1,
            )
            right = right_parts(solved, 0)
            right = jnp.concatenate([right, jnp.zeros((128 - 6 * PANEL, right.shape[1]), BF16)], axis=0)
            parts_ref[:, : (width + 1) * 128] = right
            for g in range(2):
                sums = [below[g], None]
                for j in range(PANEL):
                    other = jnp.broadcast_to(rows[0][j // 8][j % 8 : j % 8 + 1, :], (8, 128))
                    term = under[j][g] * other
                    k = j % 2
                    sums[k] = -term if sums[k] is None else sums[k] - term
                low_rows = slice(first + PANEL + 8 * g, first + PANEL + 8 * g + 8)
                a_ref[low_rows, tile(t)] = sums[0] + sums[1]
            lose(after, column_parts(jnp.concatenate(below, axis=0), p * PANEL, None), right, 1)
    while work:
        work.pop(0)()


def whiten_kernel(
    scale, gram_ref, smooth_ref, scores_ref, a_ref, w_ref, parts_ref, wp_ref, up_ref, left_ref, scores, load_sem, out_sems
):
    load = pltpu.make_async_copy(smooth_ref, left_ref, load_sem)
    load.start()
    for n, (i, j) in enumerate(BLOCKS):
        a_ref[tile(i), tile(j)] = gram_ref[tile(n), :]
    size = left_ref.shape[0] // PIECES
    copies = []

    def solve(t, n):
        here = slice(n * size, (n + 1) * size)
        value = lax.dot_general(
            left_parts(left_ref[here, tile(t)], 1),
            wp_ref[t],
            (((1,), (1,)), ((), ())),
            preferred_element_type=F32,
        )
        scores[here, tile(t)] = value * scale
        if t < 3:
            behind = (3 - t) * 128
            left_ref[here, (t + 1) * 128 :] -= dot(left_parts(value, 1), up_ref[t, :, :behind])
        copy = pltpu.make_async_copy(
            scores.at[here, tile(t)], scores_ref.at[here, tile(t)], out_sems.at[t, n]
        )
        copy.start()
        copies.append(copy)

    row = lax.broadcasted_iota(jnp.int32, (128, 128), 0)
    lane = lax.broadcasted_iota(jnp.int32, (128, 128), 1)
    identity = jnp.where(row == lane, 1.0, 0.0).astype(F32)
    work = []
    for t in range(4):
        w_ref[tile(t), :] = identity
        factor_block(t, a_ref, w_ref, parts_ref, work)
        if t == 0:
            load.wait()
        wp_ref[t] = right_parts(w_ref[tile(t), :], 1)
        if t < 3:
            behind = (3 - t) * 128
            up_ref[t, :, :behind] = right_parts(a_ref[tile(t), (t + 1) * 128 :], 0)

            def trail(s, t=t):
                a_ref[tile(s), s * 128 :] -= dot(
                    left_parts(a_ref[tile(t), tile(s)].T, 1),
                    up_ref[t, :, (s - t - 1) * 128 : (3 - t) * 128],
                )

            trail(t + 1)
            work += [functools.partial(trail, s) for s in range(t + 2, 4)]
        work += [functools.partial(solve, t, n) for n in range(PIECES)]
    while work:
        work.pop(0)()
    for copy in copies:
        copy.wait()


def whiten_call(gram, smooth, scale):
    rows = smooth.shape[0]

    def kernel(*refs):
        whiten_kernel(scale, *refs)

    return pl.pallas_call(
        kernel,
        out_shape=jax.ShapeDtypeStruct((rows, BINS), F32),
        in_specs=[
            pl.BlockSpec(memory_space=pltpu.VMEM),
            pl.BlockSpec(memory_space=pl.ANY),
        ],
        out_specs=pl.BlockSpec(memory_space=pl.ANY),
        scratch_shapes=[
            pltpu.VMEM((BINS, BINS), F32),
            pltpu.VMEM((BINS, 128), F32),
            pltpu.VMEM((128, 5 * 128), BF16),
            pltpu.VMEM((4, 128, 6 * 128), BF16),
            pltpu.VMEM((3, 6 * 128, 3 * 128), BF16),
            pltpu.VMEM((rows, BINS), F32),
            pltpu.VMEM((rows, BINS), F32),
            pltpu.SemaphoreType.DMA,
            pltpu.SemaphoreType.DMA((4, PIECES)),
        ],
        compiler_params=pltpu.CompilerParams(vmem_limit_bytes=62 << 20),
    )(gram, smooth)


def local(counts, spread):
    gram, smooth = gram_call(counts, spread.reshape(1, BINS))
    rows_all = smooth.shape[0] * lax.axis_size("gx") * lax.axis_size("gy")
    scores = whiten_call(gram, smooth, math.sqrt(rows_all))
    return scores.reshape(counts.shape)


def solution(mesh):
    in_specs = (P(None, "gx", "gy", None), P())
    out_specs = P(None, "gx", "gy", None)
    return jax.shard_map(local, mesh=mesh, in_specs=in_specs, out_specs=out_specs, check_vma=False)
```

```python
import functools
import math

import jax
import jax.numpy as jnp
from jax import lax
from jax.experimental import pallas as pl
from jax.experimental.pallas import tpu as pltpu
from jax.sharding import PartitionSpec as P

RADIUS = 2
BINS = 512
PLANES = 4
SIDE = 16
CORES = 2
X_CHIPS = 4
Y_CHIPS = 8
Z_CHIPS = 8
F32 = jnp.float32
BF16 = jnp.bfloat16
MESH = pl.DeviceIdType.MESH

BLOCKS = [(i, j) for i in range(4) for j in range(i, 4)]
PACKED = len(BLOCKS) * 128
CHUNKS = [(0, 512), (512, PACKED - 512)]


def shares(rows):
    half = rows // CORES
    quarter = half // X_CHIPS
    eighth = -(-quarter // (8 * Z_CHIPS)) * 8
    return half, quarter, eighth


PANEL = 16
PIECES = 8


def split3(x):
    high = x.astype(BF16)
    rest = x - high.astype(F32)
    middle = rest.astype(BF16)
    return high, middle, (rest - middle.astype(F32)).astype(BF16)


def left_parts(x, axis):
    high, middle, low = split3(x)
    return jnp.concatenate([high, high, middle, high, low, middle], axis=axis)


def right_parts(x, axis):
    high, middle, low = split3(x)
    return jnp.concatenate([high, middle, high, low, high, middle], axis=axis)


def tile(s):
    return slice(s * 128, s * 128 + 128)


def dot(left, right):
    return jnp.dot(left, right, preferred_element_type=F32)


def tap_rows(spread):
    offsets = [float(k) for k in range(-RADIUS, RADIUS + 1)]
    profile = [jnp.exp(-k * k / (2.0 * spread * spread)) for k in offsets]
    total = profile[0]
    for row in profile[1:]:
        total = total + row
    return [row / total for row in profile]


def gram_kernel(
    counts_ref,
    spread_ref,
    gram_ref,
    smooth_ref,
    grid,
    blurred,
    smooth,
    edge_out,
    edge_in,
    corner_out,
    corner_in,
    packed,
    from_core0,
    from_x0,
    quarter0,
    from_z0,
    from_y0,
    gathered0,
    from_core1,
    from_x1,
    quarter1,
    from_z1,
    from_y1,
    gathered1,
    whole,
    taps_in,
    load_sems,
    taps_sem,
    x_send,
    x_recv,
    y_send,
    y_recv,
    c_send,
    c_recv,
    red_send,
    red_recv,
    out_sems,
):
    gx, gy = lax.axis_index("gx"), lax.axis_index("gy")
    nx, ny = CORES * Y_CHIPS, Z_CHIPS * X_CHIPS
    core, y = lax.rem(gx, CORES), gx // CORES
    x, z = lax.rem(gy, X_CHIPS), gy // X_CHIPS

    taps_load = pltpu.make_async_copy(spread_ref, taps_in, taps_sem)
    taps_load.start()
    loads = []
    for p in range(PLANES):
        load = pltpu.make_async_copy(
            counts_ref.at[p],
            grid.at[p, RADIUS : RADIUS + SIDE, 8 : 8 + SIDE, :],
            load_sems.at[p],
        )
        load.start()
        loads.append(load)

    def core_peer():
        return (y * CORES + 1 - core, gy)

    def x_peer(d):
        return (gx, z * X_CHIPS + lax.rem(x + d, X_CHIPS))

    def z_peer(d):
        return (gx, lax.rem(z + d, Z_CHIPS) * X_CHIPS + x)

    def y_peer(d):
        return (lax.rem(y + d, Y_CHIPS) * CORES + core, gy)

    def beside(dx, dy):
        return (lax.rem(gx + dx + nx, nx), lax.rem(gy + dy + ny, ny))

    around = [(dx, dy) for dx in (-1, 0, 1) for dy in (-1, 0, 1) if (dx, dy) != (0, 0)]
    partners = [beside(dx, dy) for dx, dy in around]
    partners += [core_peer()]
    partners += [x_peer(d) for d in range(1, X_CHIPS)]
    partners += [z_peer(d) for d in range(1, Z_CHIPS)]
    partners += [y_peer(d) for d in range(1, Y_CHIPS)]
    barrier = pltpu.get_barrier_semaphore()
    for partner in partners:
        pl.semaphore_signal(barrier, inc=1, device_id=partner, device_id_type=MESH)

    def there(dx, dy):
        inside = None
        for delta, here, size in ((dx, gx, nx), (dy, gy, ny)):
            if delta:
                test = here > 0 if delta < 0 else here < size - 1
                inside = test if inside is None else jnp.logical_and(inside, test)
        return inside

    for p in range(PLANES):
        loads[p].wait()
        for i in range(SIDE):
            row = grid[p, RADIUS + i, 8:16, :]
            edge_out[0, p, 2 * i : 2 * i + 2, :] = row[0:2]
            row2 = grid[p, RADIUS + i, 16:24, :]
            edge_out[1, p, 2 * i : 2 * i + 2, :] = row2[6:8]
        for a, first in ((0, 0), (1, SIDE - 2)):
            for b in (0, 1):
                corner_out[2 * a + b, 4 * p : 4 * p + 4, :] = edge_out[
                    b, p, 2 * first : 2 * first + 4, :
                ]

    pl.semaphore_wait(barrier, len(partners))

    def x_copy(p, side):
        rows = (RADIUS, RADIUS + SIDE - 2)[side]
        lands = (RADIUS + SIDE, 0)[side]
        return pltpu.make_async_remote_copy(
            src_ref=grid.at[p, rows : rows + 2, 8 : 8 + SIDE, :],
            dst_ref=grid.at[p, lands : lands + 2, 8 : 8 + SIDE, :],
            send_sem=x_send.at[p, side],
            recv_sem=x_recv.at[p, side],
            device_id=beside((-1, 1)[side], 0),
            device_id_type=MESH,
        )

    def y_copy(p, side):
        return pltpu.make_async_remote_copy(
            src_ref=edge_out.at[side, p],
            dst_ref=edge_in.at[1 - side, p],
            send_sem=y_send.at[p, side],
            recv_sem=y_recv.at[p, side],
            device_id=beside(0, (-1, 1)[side]),
            device_id_type=MESH,
        )

    def corner_copy(a, b):
        return pltpu.make_async_remote_copy(
            src_ref=corner_out.at[2 * a + b],
            dst_ref=corner_in.at[2 * (1 - a) + 1 - b],
            send_sem=c_send.at[2 * a + b],
            recv_sem=c_recv.at[2 * a + b],
            device_id=beside((-1, 1)[a], (-1, 1)[b]),
            device_id_type=MESH,
        )

    sign = (-1, 1)
    for a in (0, 1):
        for b in (0, 1):

            @pl.when(there(sign[a], sign[b]))
            def _():
                corner_copy(a, b).start()

            @pl.when(jnp.logical_not(there(sign[a], sign[b])))
            def _():
                corner_in[2 * a + b] = jnp.zeros((4 * PLANES, BINS), F32)

    for p in range(PLANES):
        for side in (0, 1):

            @pl.when(there(0, sign[side]))
            def _():
                y_copy(p, side).start()

            @pl.when(there(sign[side], 0))
            def _():
                x_copy(p, side).start()

    for side in (0, 1):

        @pl.when(jnp.logical_not(there(0, sign[side])))
        def _():
            edge_in[side] = jnp.zeros((PLANES, 2 * SIDE, BINS), F32)

        @pl.when(jnp.logical_not(there(sign[side], 0)))
        def _():
            lands = (0, RADIUS + SIDE)[side]
            for p in range(PLANES):
                grid[p, lands : lands + 2, 8 : 8 + SIDE, :] = jnp.zeros((2, SIDE, BINS), F32)

    taps_load.wait()
    taps = tap_rows(taps_in[...])

    def along_x(p, i, lo, hi):
        total = taps[0] * grid[p, i, lo:hi, :]
        for k in range(1, 2 * RADIUS + 1):
            total = total + taps[k] * grid[p, i + k, lo:hi, :]
        blurred[p, i, lo:hi, :] = total

    for p in range(PLANES):

        def inner_x(i, carry, p=p):
            along_x(p, i, 8, 8 + SIDE)
            return carry

        lax.fori_loop(RADIUS, SIDE - RADIUS, inner_x, 0)

    for a in (0, 1):
        for b in (0, 1):

            @pl.when(there(sign[1 - a], sign[1 - b]))
            def _():
                corner_copy(a, b).wait_recv()

    def rows_at(start, size):
        return pl.ds(pl.multiple_of(start, 8), size)

    buffers = [
        (from_core0, from_x0, quarter0, from_z0, from_y0, gathered0),
        (from_core1, from_x1, quarter1, from_z1, from_y1, gathered1),
    ]
    leaves = []
    gives = []

    def reduction(c):
        first, rows = CHUNKS[c]
        half, fourth, eighth = shares(rows)
        from_core, from_x, quarter, from_z, from_y, gathered = buffers[c]

        def send(step, source, target, device):
            pltpu.make_async_remote_copy(
                src_ref=source,
                dst_ref=target,
                send_sem=red_send.at[c, step],
                recv_sem=red_recv.at[c, step],
                device_id=device,
                device_id_type=MESH,
            ).start()

        def arrived(step, landed):
            pltpu.make_async_copy(landed, landed, red_recv.at[c, step]).wait()

        def left(step, gone):
            leaves.append(lambda: pltpu.make_async_copy(gone, gone, red_send.at[c, step]).wait())

        send(0, packed.at[rows_at(first + (1 - core) * half, half)], from_core, core_peer())
        left(0, from_core)
        if fourth < Z_CHIPS * eighth:
            quarter[fourth:, :] = jnp.zeros((Z_CHIPS * eighth - fourth, 128), F32)
        yield
        arrived(0, from_core)
        mine = first + core * half
        packed[rows_at(mine, half), :] += from_core[...]

        for d in range(1, X_CHIPS):
            send(
                1,
                packed.at[rows_at(mine + lax.rem(x + d, X_CHIPS) * fourth, fourth)],
                from_x.at[d - 1],
                x_peer(d),
            )
        left(1, from_x)
        yield
        arrived(1, from_x)
        total = packed[rows_at(mine + x * fourth, fourth), :]
        for d in range(X_CHIPS - 1):
            total = total + from_x[d]
        quarter[0:fourth, :] = total

        for d in (4, 3, 5, 2, 6, 1, 7):
            send(
                2,
                quarter.at[rows_at(lax.rem(z + d, Z_CHIPS) * eighth, eighth)],
                from_z.at[d - 1],
                z_peer(d),
            )
        left(2, from_z)
        yield
        arrived(2, from_z)
        total = quarter[rows_at(z * eighth, eighth), :]
        for d in range(Z_CHIPS - 1):
            total = total + from_z[d]

        from_y[y] = total
        for d in (4, 3, 5, 2, 6, 1, 7):
            send(3, from_y.at[y], from_y.at[y], y_peer(d))
        left(3, from_y.at[1:])
        yield
        arrived(3, from_y.at[1:])
        total = from_y[0]
        for d in range(1, Y_CHIPS):
            total = total + from_y[d]

        here = rows_at(z * eighth, eighth)
        gathered[here, :] = total
        for d in (4, 3, 5, 2, 6, 1, 7):
            send(4, gathered.at[here], gathered.at[here], z_peer(d))
        left(4, gathered.at[eighth:])
        yield
        arrived(4, gathered.at[eighth:])
        here = rows_at(mine + x * fourth, fourth)
        for d in range(1, X_CHIPS):
            send(5, gathered.at[0:fourth], whole.at[here], x_peer(d))
        left(5, from_x)
        whole[here, :] = gathered[0:fourth, :]
        yield
        arrived(5, from_x)
        here = rows_at(mine, half)
        send(6, whole.at[here], whole.at[here], core_peer())
        left(6, from_core)
        yield
        arrived(6, from_core)
        give = pltpu.make_async_copy(
            whole.at[first : first + rows], gram_ref.at[first : first + rows], out_sems.at[PLANES + c]
        )
        give.start()
        gives.append(give)

    keeps = []
    for p in range(PLANES):
        for side in (0, 1):

            @pl.when(there(0, sign[1 - side]))
            def _():
                y_copy(p, side).wait_recv()

            @pl.when(there(sign[1 - side], 0))
            def _():
                x_copy(p, side).wait_recv()

        for b, lands in ((0, 6), (1, 8 + SIDE)):
            for i in range(SIDE):
                grid[p, RADIUS + i, lands : lands + 2, :] = edge_in[b, p, 2 * i : 2 * i + 2, :]
            for a, first in ((0, 0), (1, RADIUS + SIDE)):
                for i in (0, 1):
                    grid[p, first + i, lands : lands + 2, :] = corner_in[
                        2 * a + b, 4 * p + 2 * i : 4 * p + 2 * i + 2, :
                    ]

        def beside_x(i, carry, p=p):
            along_x(p, i, 0, 8)
            along_x(p, i, 8 + SIDE, 16 + SIDE)
            return carry

        lax.fori_loop(0, SIDE, beside_x, 0)
        for i in (0, 1, SIDE - 2, SIDE - 1):
            along_x(p, i, 8, 8 + SIDE)

        def along_y(i, carry, p=p):
            total = taps[0] * blurred[p, i, 6 : 6 + SIDE, :]
            for k in range(1, 2 * RADIUS + 1):
                total = total + taps[k] * blurred[p, i, 6 + k : 6 + k + SIDE, :]
            at = pl.multiple_of(p * SIDE * SIDE + i * SIDE, SIDE)
            smooth[pl.ds(at, SIDE), :] = total
            return carry

        lax.fori_loop(0, SIDE, along_y, 0)
        rows = slice(p * SIDE * SIDE, (p + 1) * SIDE * SIDE)
        keep = pltpu.make_async_copy(smooth.at[rows], smooth_ref.at[rows], out_sems.at[p])
        keep.start()
        keeps.append(keep)

        value = smooth[rows, :]
        high, middle, _ = split3(value.T)
        left = jnp.concatenate([high, high, middle, middle], axis=1)
        high, middle, _ = split3(value)
        right = jnp.concatenate([high, middle, high, middle], axis=0)
        at = 0
        for i in range(4):
            part = dot(left[tile(i), :], right[:, i * 128 :])
            for j in range(4 - i):
                block = part[:, tile(j)]
                if p == 0:
                    packed[at : at + 128, :] = block
                else:
                    packed[at : at + 128, :] += block
                at += 128
            if p == PLANES - 1 and i == 0:
                first_chunk = reduction(0)
                next(first_chunk)

    second_chunk = reduction(1)
    next(second_chunk)
    for p in range(PLANES):
        for side in (0, 1):

            @pl.when(there(0, sign[side]))
            def _():
                y_copy(p, side).wait_send()

            @pl.when(there(sign[side], 0))
            def _():
                x_copy(p, side).wait_send()

        keeps[p].wait()
    for a in (0, 1):
        for b in (0, 1):

            @pl.when(there(sign[a], sign[b]))
            def _():
                corner_copy(a, b).wait_send()

    under_way = [first_chunk, second_chunk]
    while under_way:
        under_way = [chunk for chunk in under_way if next(chunk, chunk) is not chunk]
    for wait in leaves:
        wait()
    for give in gives:
        give.wait()


def gram_call(counts, spread):
    dma = pltpu.SemaphoreType.DMA
    rows = PLANES * SIDE * SIDE
    reduction_buffers = []
    for _, chunk in CHUNKS:
        half, fourth, eighth = shares(chunk)
        for shape in (
            (half,),
            (X_CHIPS - 1, fourth),
            (Z_CHIPS * eighth,),
            (Z_CHIPS - 1, eighth),
            (Y_CHIPS, eighth),
            (Z_CHIPS * eighth,),
        ):
            reduction_buffers.append(pltpu.VMEM((*shape, 128), F32))
    return pl.pallas_call(
        gram_kernel,
        out_shape=[
            jax.ShapeDtypeStruct((PACKED, 128), F32),
            jax.ShapeDtypeStruct((rows, BINS), F32),
        ],
        in_specs=[pl.BlockSpec(memory_space=pl.ANY)] * 2,
        out_specs=[pl.BlockSpec(memory_space=pl.ANY)] * 2,
        scratch_shapes=[
            pltpu.VMEM((PLANES, SIDE + 2 * RADIUS, SIDE + 16, BINS), F32),
            pltpu.VMEM((PLANES, SIDE, SIDE + 16, BINS), F32),
            pltpu.VMEM((rows, BINS), F32),
            pltpu.VMEM((2, PLANES, 2 * SIDE, BINS), F32),
            pltpu.VMEM((2, PLANES, 2 * SIDE, BINS), F32),
            pltpu.VMEM((4, 4 * PLANES, BINS), F32),
            pltpu.VMEM((4, 4 * PLANES, BINS), F32),
            pltpu.VMEM((PACKED, 128), F32),
            *reduction_buffers,
            pltpu.VMEM((PACKED, 128), F32),
            pltpu.VMEM((1, BINS), F32),
            dma((PLANES,)),
            dma,
            dma((PLANES, 2)),
            dma((PLANES, 2)),
            dma((PLANES, 2)),
            dma((PLANES, 2)),
            dma((4,)),
            dma((4,)),
            dma((2, 7)),
            dma((2, 7)),
            dma((PLANES + 2,)),
        ],
        compiler_params=pltpu.CompilerParams(
            collective_id=0, has_side_effects=True, vmem_limit_bytes=62 << 20
        ),
    )(counts, spread)


def factor_block(t, a_ref, w_ref, parts_ref, work):
    sublane = lax.broadcasted_iota(jnp.int32, (8, 128), 0)
    panels = 128 // PANEL
    width = 4 - t

    def at(s, rows):
        return (a_ref, rows, tile(t + s)) if s < width else (w_ref, rows, slice(0, 128))

    def column_parts(value, first, keep):
        lane = lax.broadcasted_iota(jnp.int32, value.shape, 1)
        column = jnp.take_along_axis(value, first + lane % PANEL, axis=1)
        if keep is not None:
            column = jnp.where(keep, column, 0.0)
        high, middle, low = split3(column)
        high, middle, low = high.astype(F32), middle.astype(F32), low.astype(F32)
        group = lane // PANEL
        value = jnp.where(
            (group == 0) | (group == 1) | (group == 3),
            high,
            jnp.where((group == 2) | (group == 5), middle, jnp.where(group == 4, low, 0.0)),
        )
        return value.astype(BF16)

    def lose(rows, left, right, skip=0):
        update = dot(left, right[:, skip * 128 :])
        for s in range(skip, width + 1):
            ref, at_rows, columns = at(s, rows)
            ref[at_rows, columns] -= update[:, tile(s - skip)]

    for p in range(panels):
        first = t * 128 + p * PANEL
        here = slice(first, first + PANEL)
        rows = []
        for s in range(width + 1):
            ref, at_rows, columns = at(s, here)
            rows.append([ref[first + 8 * g : first + 8 * g + 8, columns] for g in range(2)])
        column = [
            [
                jnp.take_along_axis(
                    rows[0][g], jnp.full((8, 128), p * PANEL + j, jnp.int32), axis=1
                )
                for g in range(2)
            ]
            for j in range(PANEL)
        ]
        factor = [list(value) for value in rows]
        pivots = [jnp.ones((8, 128), F32)] * 2
        inverses = [jnp.ones((8, 128), F32)] * 2
        if 0 < p < panels - 1:
            beyond = slice(first + PANEL, t * 128 + 128)
            left = column_parts(a_ref[beyond, tile(t)], (p - 1) * PANEL, None)
            lose(beyond, left, parts_ref[:, : (width + 1) * 128])
        if p < panels - 1:
            after = slice(first + PANEL, first + 2 * PANEL)
            below = [a_ref[first + PANEL + 8 * g : first + PANEL + 8 * g + 8, tile(t)] for g in range(2)]
        under = []
        for j in range(PANEL):
            h, q = divmod(j, 8)
            pivot = jnp.broadcast_to(column[j][h][q : q + 1, :], (8, 128))
            inverse = 1.0 / pivot
            pivots[h] = jnp.where(sublane == q, pivot, pivots[h])
            inverses[h] = jnp.where(sublane == q, inverse, inverses[h])
            if p < panels - 1:
                at_lane = jnp.full((8, 128), p * PANEL + j, jnp.int32)
                under.append([jnp.take_along_axis(value, at_lane, axis=1) * inverse for value in below])
            weight = [
                (jnp.where(sublane != q, column[j][g], 0.0) if g == h else column[j][g]) * inverse
                for g in range(2)
            ]
            for i in range(j + 1, PANEL):
                other = jnp.broadcast_to(column[i][h][q : q + 1, :], (8, 128))
                for g in range(2):
                    column[i][g] = column[i][g] - weight[g] * other
            for value, kept in zip(rows, factor):
                other = jnp.broadcast_to(value[h][q : q + 1, :], (8, 128))
                kept[h] = jnp.where(sublane == q, other, kept[h])
                for g in range(2):
                    value[g] = value[g] - weight[g] * other
            if (j == 6 or (j == 12 and p < 2)) and work:
                work.pop(0)()
        scale = [lax.rsqrt(value) for value in pivots]
        for s, kept in enumerate(factor):
            ref, at_rows, columns = at(s, here)
            ref[at_rows, columns] = jnp.concatenate([kept[g] * scale[g] for g in range(2)], axis=0)
        if p < panels - 1:
            solved = jnp.concatenate(
                [
                    jnp.concatenate([value[g] * inverses[g] for g in range(2)], axis=0)
                    for value in rows
                ],
                axis=1,
            )
            right = right_parts(solved, 0)
            right = jnp.concatenate([right, jnp.zeros((128 - 6 * PANEL, right.shape[1]), BF16)], axis=0)
            parts_ref[:, : (width + 1) * 128] = right
            for g in range(2):
                sums = [below[g], None]
                for j in range(PANEL):
                    other = jnp.broadcast_to(rows[0][j // 8][j % 8 : j % 8 + 1, :], (8, 128))
                    term = under[j][g] * other
                    k = j % 2
                    sums[k] = -term if sums[k] is None else sums[k] - term
                low_rows = slice(first + PANEL + 8 * g, first + PANEL + 8 * g + 8)
                a_ref[low_rows, tile(t)] = sums[0] + sums[1]
            lose(after, column_parts(jnp.concatenate(below, axis=0), p * PANEL, None), right, 1)
    while work:
        work.pop(0)()


def whiten_kernel(
    scale, gram_ref, smooth_ref, scores_ref, a_ref, w_ref, parts_ref, wp_ref, up_ref, left_ref, scores, load_sem, block_sems, out_sems
):
    blocks = []
    for n, (i, j) in enumerate(BLOCKS):
        block = pltpu.make_async_copy(
            gram_ref.at[tile(n), :], a_ref.at[tile(i), tile(j)], block_sems.at[n]
        )
        block.start()
        blocks.append(block)
    load = pltpu.make_async_copy(smooth_ref, left_ref, load_sem)
    load.start()
    size = left_ref.shape[0] // PIECES
    copies = []

    def solve(t, n):
        here = slice(n * size, (n + 1) * size)
        value = lax.dot_general(
            left_parts(left_ref[here, tile(t)], 1),
            wp_ref[t],
            (((1,), (1,)), ((), ())),
            preferred_element_type=F32,
        )
        scores[here, tile(t)] = value * scale
        if t < 3:
            behind = (3 - t) * 128
            left_ref[here, (t + 1) * 128 :] -= dot(left_parts(value, 1), up_ref[t, :, :behind])
        copy = pltpu.make_async_copy(
            scores.at[here, tile(t)], scores_ref.at[here, tile(t)], out_sems.at[t, n]
        )
        copy.start()
        copies.append(copy)

    row = lax.broadcasted_iota(jnp.int32, (128, 128), 0)
    lane = lax.broadcasted_iota(jnp.int32, (128, 128), 1)
    identity = jnp.where(row == lane, 1.0, 0.0).astype(F32)
    work = []
    for t in range(4):
        w_ref[tile(t), :] = identity
        if t == 0:
            for block in blocks[:4]:
                block.wait()
        factor_block(t, a_ref, w_ref, parts_ref, work)
        if t == 0:
            for block in blocks[4:]:
                block.wait()
            load.wait()
        wp_ref[t] = right_parts(w_ref[tile(t), :], 1)
        if t < 3:
            behind = (3 - t) * 128
            up_ref[t, :, :behind] = right_parts(a_ref[tile(t), (t + 1) * 128 :], 0)

            def trail(s, t=t):
                a_ref[tile(s), s * 128 :] -= dot(
                    left_parts(a_ref[tile(t), tile(s)].T, 1),
                    up_ref[t, :, (s - t - 1) * 128 : (3 - t) * 128],
                )

            trail(t + 1)
            work += [functools.partial(trail, s) for s in range(t + 2, 4)]
        work += [functools.partial(solve, t, n) for n in range(PIECES)]
    while work:
        work.pop(0)()
    for copy in copies:
        copy.wait()


def whiten_call(gram, smooth, scale):
    rows = smooth.shape[0]

    def kernel(*refs):
        whiten_kernel(scale, *refs)

    return pl.pallas_call(
        kernel,
        out_shape=jax.ShapeDtypeStruct((rows, BINS), F32),
        in_specs=[pl.BlockSpec(memory_space=pl.ANY)] * 2,
        out_specs=pl.BlockSpec(memory_space=pl.ANY),
        scratch_shapes=[
            pltpu.VMEM((BINS, BINS), F32),
            pltpu.VMEM((BINS, 128), F32),
            pltpu.VMEM((128, 5 * 128), BF16),
            pltpu.VMEM((4, 128, 6 * 128), BF16),
            pltpu.VMEM((3, 6 * 128, 3 * 128), BF16),
            pltpu.VMEM((rows, BINS), F32),
            pltpu.VMEM((rows, BINS), F32),
            pltpu.SemaphoreType.DMA,
            pltpu.SemaphoreType.DMA((len(BLOCKS),)),
            pltpu.SemaphoreType.DMA((4, PIECES)),
        ],
        compiler_params=pltpu.CompilerParams(vmem_limit_bytes=62 << 20),
    )(gram, smooth)


def local(counts, spread):
    gram, smooth = gram_call(counts, spread.reshape(1, BINS))
    rows_all = smooth.shape[0] * lax.axis_size("gx") * lax.axis_size("gy")
    scores = whiten_call(gram, smooth, math.sqrt(rows_all))
    return scores.reshape(counts.shape)


def solution(mesh):
    in_specs = (P(None, "gx", "gy", None), P())
    out_specs = P(None, "gx", "gy", None)
    return jax.shard_map(local, mesh=mesh, in_specs=in_specs, out_specs=out_specs, check_vma=False)
```
